32 devices in a mesh: phase: 8 (over y, x, core), chan: 4 (over z).
Axes of the slice: x: 2, y: 2, z: 4, core: 2. Of those that a mesh axis runs over, the one named last changes fastest.
Arguments:
- frames: bfloat16 [64, 16, 512], P(None, 'phase', 'chan'), may hold values from -6 to 6
- temporal_taps: float32 [4, 3, 64], replicated, may hold values from -3 to 3
- conv_weights: bfloat16 [4, 64, 27, 2, 64], P(None, None, None, None, 'chan'), may hold values from -0.15625 to 0.15625
- cotangent: bfloat16 [64, 16, 512], P(None, 'phase', 'chan'), may hold values from -16 to 16
Outputs:
- final_frames: bfloat16 [64, 16, 512], P(None, 'phase', 'chan')
- grad_frames: bfloat16 [64, 16, 512], P(None, 'phase', 'chan')
- grad_taps: float32 [4, 3, 64], replicated
- grad_weights: float32 [4, 64, 27, 2, 64], P(None, None, None, None, 'chan')
The draws below stay inside these ranges and needn't reach their ends.
All inputs are finite; a program needn't handle non-finite values.
Results may differ from the reference program's by a relative error of at most 0.025.
Values may be sent and summed in bfloat16 or wider, within the bound.
A program may use at most 64 MiB of HBM per device.

```python
import jax
import jax.numpy as jnp
from jax import lax

C = 64
BLOCKS = 4
SY = 8
SZ = 16
SX = 4
V = 512
PHASES = 16


def draw_cotangent(key, part):
    base = jax.random.normal(key, (C, PHASES, V), jnp.float32)
    phase_pos = jnp.arange(PHASES, dtype=jnp.float32) / max(PHASES - 1, 1)
    plane_pos = (jnp.arange(V, dtype=jnp.int32) // (SY * SZ)).astype(jnp.float32) / max(SX - 1, 1)
    scale = 0.5 * (1.0 + 2.0 * phase_pos)[:, None] * (1.0 + 2.0 * plane_pos)[None, :]
    return jnp.clip(base * scale[None, :, :], -16.0, 16.0).astype(jnp.bfloat16)


def shard_levels(key, extent, pieces, smallest, high):
    def one(dim, shards_of):
        heights = jax.random.uniform(jax.random.fold_in(jax.random.fold_in(key, 6), dim), (shards_of,), jnp.float32, smallest / len(pieces), high / len(pieces))
        return jnp.repeat(jnp.exp(heights), extent[dim] // shards_of).reshape((-1,) + (1,) * (len(extent) - dim - 1))

    gain = one(*pieces[0])
    for cut in pieces[1:]:
        gain = gain * one(*cut)
    return gain


def bell_draw(key, shape, scale, most, cuts=(), kind=jnp.bfloat16):
    array = jax.random.normal(key, shape, jnp.float32) * scale
    if len(cuts) > 0:
        array = shard_levels(key, shape, cuts, -0.22, 0.18) * array
    return jnp.clip(array, min=-most, max=most).astype(kind)


def setup_inputs(seed: int = 0) -> dict:
    splits = jax.random.split(jax.random.key(seed), 5)
    frames = bell_draw(splits[0], (C, PHASES, V), 1.0, 6.0, ((1, 8), (2, 4)))
    temporal_taps = bell_draw(splits[1], (BLOCKS, 3, C), 0.6, 3.0, (), jnp.float32)
    conv_weights = bell_draw(splits[2], (BLOCKS, C, 27, 2, C), (27 * C) ** -0.5, 0.15625, ((4, 4),))
    cotangent = draw_cotangent(jax.random.fold_in(splits[4], 71), 0)
    return dict(frames=frames, temporal_taps=temporal_taps, conv_weights=conv_weights, cotangent=cotangent)


def conv_cells(mixed, kernel):
    chans = mixed.shape[0]
    phases = mixed.shape[1]
    lhs = jnp.transpose(mixed, (1, 0, 2)).reshape(phases, chans, SX, SY, SZ)
    kern = kernel.reshape(chans, 3, 3, 3, 2 * chans)
    kern = jnp.transpose(kern, (4, 0, 1, 2, 3))
    result = lax.conv_general_dilated(lhs, kern, (1, 1, 1), [(1, 1), (1, 1), (1, 1)], dimension_numbers=('NCDHW', 'OIDHW', 'NCDHW'), precision=lax.Precision.HIGHEST)
    result = result.reshape(phases, 2, chans, SX * SY * SZ)
    return jnp.transpose(result, (2, 1, 0, 3))

def reference(frames, temporal_taps, conv_weights, cotangent):
    state = frames
    saved = []
    for block_num in range(BLOCKS):
        reach = 2 ** block_num
        behind = jnp.roll(state, reach, axis=1)
        ahead = jnp.roll(state, -reach, axis=1)
        tap_rows = temporal_taps[block_num][:, :, None, None]
        mixed = (tap_rows[0] * behind.astype(jnp.float32) + tap_rows[1] * state.astype(jnp.float32) + tap_rows[2] * ahead.astype(jnp.float32)).astype(jnp.bfloat16)
        conv_out = conv_cells(mixed.astype(jnp.float32), conv_weights[block_num].astype(jnp.float32))
        value_part = conv_out[:, 0]
        gate_sig = jax.nn.sigmoid(conv_out[:, 1])
        saved.append((state, behind, ahead, mixed, value_part, gate_sig))
        state = (state.astype(jnp.float32) + value_part * gate_sig).astype(jnp.bfloat16)
    grad_state = cotangent
    weight_grads = [None] * BLOCKS
    tap_grads = [None] * BLOCKS
    for block_num in reversed(range(BLOCKS)):
        reach = 2 ** block_num
        prior, behind, ahead, mixed, value_part, gate_sig = saved[block_num]
        tap_rows = temporal_taps[block_num][:, :, None, None]
        grad_y = grad_state.astype(jnp.float32)
        grad_z = jnp.stack([grad_y * gate_sig, grad_y * value_part * gate_sig * (1.0 - gate_sig)], axis=1).astype(jnp.bfloat16)
        outputs_now, pullback = jax.vjp(conv_cells, mixed.astype(jnp.float32), conv_weights[block_num].astype(jnp.float32))
        grad_mix, grad_kernel = pullback(grad_z.astype(jnp.float32))
        grad_tap = jnp.stack([lax.optimization_barrier(jnp.sum(grad_mix * behind.astype(jnp.float32), axis=(1, 2))), lax.optimization_barrier(jnp.sum(grad_mix * prior.astype(jnp.float32), axis=(1, 2))), lax.optimization_barrier(jnp.sum(grad_mix * ahead.astype(jnp.float32), axis=(1, 2)))])
        grad_low = grad_mix.astype(jnp.bfloat16).astype(jnp.float32)
        grad_state = (grad_y + tap_rows[0] * jnp.roll(grad_low, -reach, axis=1) + tap_rows[1] * grad_low + tap_rows[2] * jnp.roll(grad_low, reach, axis=1)).astype(jnp.bfloat16)
        weight_grads[block_num] = grad_kernel
        tap_grads[block_num] = grad_tap
    return (state, grad_state, jnp.stack(tap_grads), jnp.stack(weight_grads))
```

```python
import functools

import jax
import jax.numpy as jnp
from jax import lax
from jax.experimental import pallas as pl
from jax.experimental.pallas import tpu as pltpu
from jax.sharding import PartitionSpec as P

BLOCKS = 4
SY = 8
SZ = 16


cell_offsets = [
    (kernel_pos // 9 - 1, kernel_pos // 3 % 3 - 1, kernel_pos % 3 - 1) for kernel_pos in range(27)
]


def shifted(block, axis, distance):
    devices = range(lax.axis_size(axis))
    route = [((i - distance) % len(devices), i) for i in devices]
    return lax.ppermute(block, axis, route)


def padded_2(cells, sides, width):
    for axis, dim in sides:
        count = lax.axis_size(axis)
        ends = count - 1
        head = lax.slice_in_dim(cells, 0, width, axis=dim)
        tail = lax.slice_in_dim(cells, cells.shape[dim] - width, cells.shape[dim], axis=dim)
        cells = jnp.concatenate(
            [
                lax.ppermute(tail, axis, [(i, (i + 1) % count) for i in range(ends)]),
                cells,
                lax.ppermute(head, axis, [((i + 1) % count, i) for i in range(ends)]),
            ],
            axis=dim,
        )
    return cells


def within_plane(source, step_y, step_z):
    cell_count = source.shape[-1]
    last_dim = source.ndim - 1
    margin = SZ + 1
    moved = step_y * SZ + step_z
    padded = jnp.pad(source, [(0, 0)] * last_dim + [(margin, margin)])
    window = lax.slice_in_dim(padded, margin + moved, margin + moved + cell_count, axis=last_dim)
    places = jnp.arange(cell_count, dtype=jnp.int32)
    coord_y = places // SZ + step_y
    coord_z = places % SZ + step_z
    inside = (coord_y >= 0) & (coord_y < SY) & (coord_z >= 0) & (coord_z < SZ)
    return jnp.where(inside, window, jnp.zeros_like(window))


def shifted_cells(rimmed, step_x, step_y, step_z):
    planes = rimmed.shape[-2] - 2
    rows = lax.slice_in_dim(rimmed, 1 + step_x, 1 + step_x + planes, axis=rimmed.ndim - 2)
    moved = within_plane(rows, step_y, step_z)
    return moved.reshape(moved.shape[:-2] + (planes * moved.shape[-1],))


def offset_stack(rimmed, first, count, sign):
    picked = cell_offsets[first : first + count]
    return jnp.stack(
        [
            shifted_cells(rimmed, sign * offset[0], sign * offset[1], sign * offset[2])
            for offset in picked
        ],
        axis=1,
    )


def back_block(source, hops):
    if hops == 0:
        return source
    return shifted(source, "phase", hops)


def next_block(source, hops):
    if hops == 0:
        return source
    return shifted(source, "phase", -hops)


def neighbours(source, reach):
    phase_rows = source.shape[1]
    hops, rest = divmod(reach, phase_rows)
    if rest == 0:
        return (back_block(source, hops), next_block(source, hops))
    joined = jnp.concatenate([back_block(source, hops + 1), back_block(source, hops)], axis=1)
    behind = joined[:, phase_rows - rest : 2 * phase_rows - rest]
    joined = jnp.concatenate([next_block(source, hops), next_block(source, hops + 1)], axis=1)
    ahead = joined[:, rest : rest + phase_rows]
    return (behind, ahead)


def per_device(frames, temporal_taps, conv_weights, cotangent):
    chans, phase_rows, cell_count = frames.shape
    plane_cells = SY * SZ
    planes = cell_count // plane_cells
    state = frames
    saved = []
    for block_num in range(BLOCKS):
        reach = 2**block_num
        behind, ahead = neighbours(state, reach)
        tap_rows = temporal_taps[block_num][:, :, None, None]
        mixed = (
            tap_rows[0] * behind.astype(jnp.float32)
            + tap_rows[1] * state.astype(jnp.float32)
            + tap_rows[2] * ahead.astype(jnp.float32)
        ).astype(jnp.bfloat16)
        rimmed = padded_2(mixed.reshape(chans, phase_rows, planes, plane_cells), (("chan", 2),), 1)
        kernel = lax.all_gather(conv_weights[block_num], "chan", axis=3, tiled=True)
        conv_out = jnp.zeros((chans, 2, phase_rows, cell_count), jnp.float32)
        for first in range(0, 27, 9):
            group = offset_stack(rimmed, first, 9, 1)
            conv_out = conv_out + jnp.einsum(
                "ikpv,ikgo->ogpv",
                group,
                kernel[:, first : first + 9],
                preferred_element_type=jnp.float32,
            )
        value_part = conv_out[:, 0]
        gate_sig = jax.nn.sigmoid(conv_out[:, 1])
        saved.append((state, behind, ahead, rimmed, kernel, value_part, gate_sig))
        state = (state.astype(jnp.float32) + value_part * gate_sig).astype(jnp.bfloat16)
    grad_state = cotangent
    weight_grads = [None] * BLOCKS
    tap_grads = [None] * BLOCKS
    for block_num in reversed(range(BLOCKS)):
        reach = 2**block_num
        prior, behind, ahead, rimmed, kernel, value_part, gate_sig = saved[block_num]
        tap_rows = temporal_taps[block_num][:, :, None, None]
        grad_y = grad_state.astype(jnp.float32)
        grad_z = jnp.stack(
            [grad_y * gate_sig, grad_y * value_part * gate_sig * (1.0 - gate_sig)], axis=1
        ).astype(jnp.bfloat16)
        rim_grad = padded_2(
            grad_z.reshape(chans, 2, phase_rows, planes, plane_cells), (("chan", 3),), 1
        )
        grad_mix = jnp.zeros((chans, phase_rows, cell_count), jnp.float32)
        for first in range(0, 27, 3):
            group = offset_stack(rim_grad, first, 3, -1)
            grad_mix = grad_mix + jnp.einsum(
                "okgpv,ikgo->ipv",
                group,
                kernel[:, first : first + 3],
                preferred_element_type=jnp.float32,
            )
        kernel_parts = []
        for first in range(0, 27, 9):
            group = offset_stack(rimmed, first, 9, 1)
            kernel_parts.append(
                jnp.einsum("ikpv,ogpv->ikgo", group, grad_z, preferred_element_type=jnp.float32)
            )
        grad_kernel = jnp.concatenate(kernel_parts, axis=1)
        grad_tap = jnp.stack(
            [
                jnp.sum(grad_mix * behind.astype(jnp.float32), axis=(1, 2)),
                jnp.sum(grad_mix * prior.astype(jnp.float32), axis=(1, 2)),
                jnp.sum(grad_mix * ahead.astype(jnp.float32), axis=(1, 2)),
            ]
        )
        grad_low = grad_mix.astype(jnp.bfloat16)
        back_mix, ahead_mix = neighbours(grad_low, reach)
        grad_state = (
            grad_y
            + tap_rows[0] * ahead_mix.astype(jnp.float32)
            + tap_rows[1] * grad_low.astype(jnp.float32)
            + tap_rows[2] * back_mix.astype(jnp.float32)
        ).astype(jnp.bfloat16)
        kernel_piece = lax.psum_scatter(
            grad_kernel.astype(jnp.bfloat16), "chan", scatter_dimension=3, tiled=True
        )
        grad_kernel = lax.psum(kernel_piece, "phase").astype(jnp.float32)
        weight_grads[block_num] = grad_kernel
        tap_grads[block_num] = grad_tap
    grad_weights = jnp.stack(weight_grads)
    grad_taps = lax.psum(jnp.stack(tap_grads), ("phase", "chan"))
    return (state, grad_state, grad_taps, grad_weights)


class Copies:
    def __init__(self, send_sems, recv_sems):
        self.send_sems = send_sems
        self.recv_sems = recv_sems
        self.started = []

    def send(self, src, dst, target):
        number = len(self.started)
        copy = pltpu.make_async_remote_copy(
            src_ref=src,
            dst_ref=dst,
            send_sem=self.send_sems.at[number],
            recv_sem=self.recv_sems.at[number],
            device_id=target,
            device_id_type=pl.DeviceIdType.MESH,
        )
        copy.start()
        self.started.append(copy)
        return copy


def copy_count(phase_n, chan_n, blocks):
    return (
        4 * (chan_n - 1)
        + blocks * (2 + (chan_n - 1))
        + blocks * ((chan_n - 1) + 2 + 2 * (phase_n - 1))
        + (phase_n - 1)
        + (chan_n - 1)
    )


def plane_shift(array, step, phase_rows):
    if step == 0:
        return array
    width = array.shape[1] // phase_rows
    cells = SY * SZ
    blank = jnp.zeros((array.shape[0], cells), array.dtype)
    pieces = []
    for row in range(phase_rows):
        base = row * width
        if step < 0:
            pieces += [blank, array[:, base : base + width - cells]]
        else:
            pieces += [array[:, base + cells : base + width], blank]
    return jnp.concatenate(pieces, axis=1)


def fused_kernel(
    dims,
    frames,
    cotangent,
    taps,
    w_fwd,
    w_bwd,
    final_out,
    grad_out,
    gw_out,
    taps_out,
    fr_x,
    cot_x,
    state,
    behind_b,
    ahead_b,
    mixed,
    stack,
    value,
    gate,
    gz_stack,
    gm_send,
    gm_full,
    gm_recv,
    gl,
    gl_back,
    gl_ahead,
    gw_send,
    gw_recv,
    tap_send,
    tap_recv,
    final_send,
    grad_send,
    send_sems,
    recv_sems,
):
    phase_n, chan_n, phase_rows, own, whole, chunk = dims
    chans = own * chan_n
    width = phase_rows * whole
    local = whole // chan_n
    cells = SY * SZ
    p = lax.axis_index("phase")
    z = lax.axis_index("chan")
    copies = Copies(send_sems, recv_sems)
    f32, b16 = jnp.float32, jnp.bfloat16

    def at_phase(hop):
        return {"phase": lax.rem(p + (hop % phase_n), phase_n), "chan": z}

    def at_chan(hop):
        return {"phase": p, "chan": lax.rem(z + (hop % chan_n), chan_n)}

    def rows_of(index):
        return pl.ds(pl.multiple_of(index * own, own), own)

    barrier = pltpu.get_barrier_semaphore()
    for hop in range(1, phase_n):
        pl.semaphore_signal(
            barrier, inc=1, device_id=at_phase(hop), device_id_type=pl.DeviceIdType.MESH
        )
    for hop in range(1, chan_n):
        pl.semaphore_signal(
            barrier, inc=1, device_id=at_chan(hop), device_id_type=pl.DeviceIdType.MESH
        )
    pl.semaphore_wait(barrier, phase_n + chan_n - 2)

    lane = lax.broadcasted_iota(jnp.int32, (1, width), 1)
    coord_z = lax.rem(lane, SZ)
    coord_y = lax.rem(lane // SZ, SY)
    steps = [(k // 3 - 1, k % 3 - 1) for k in range(9)]
    masks = {}
    for step_y, step_z in steps:
        y, w = coord_y + step_y, coord_z + step_z
        masks[step_y, step_z] = (
            ((y >= 0) & (y < SY) & (w >= 0) & (w < SZ)).astype(f32)
        )

    def cell_shifts(array, sign):
        for step_y, step_z in steps:
            step_y, step_z = sign * step_y, sign * step_z
            moved = step_y * SZ + step_z
            if moved == 0:
                yield array.astype(b16)
            else:
                rolled = pltpu.roll(array, (-moved) % width, axis=1)
                yield (rolled * masks[step_y, step_z]).astype(b16)

    def spread_rows(source, target):
        got = []
        for hop in range(1, chan_n):
            there = at_chan(hop)
            got.append(copies.send(source.at[rows_of(there["chan"])], target.at[z], there))
        target[z] = source[rows_of(z), :]
        return got

    def join_planes(parts):
        pieces = []
        for row in range(phase_rows):
            for index in range(chan_n):
                pieces.append(parts[index, :, row * local : (row + 1) * local])
        return jnp.concatenate(pieces, axis=1)

    def spread_planes(array, stage, target):
        for index in range(chan_n):
            stage[index] = jnp.concatenate(
                [
                    array[:, row * whole + index * local : row * whole + (index + 1) * local]
                    for row in range(phase_rows)
                ],
                axis=1,
            )
        got = []
        for hop in range(1, chan_n):
            there = at_chan(hop)
            got.append(copies.send(stage.at[there["chan"]], target.at[z], there))
        target[z] = stage[z]
        return got

    def start_neighbours(source, back, ahead, reach):
        hops, rest = divmod(reach, phase_rows)
        if rest:
            edge = rest * whole
            got = [
                copies.send(source.at[:, width - edge :], back.at[:, :edge], at_phase(1)),
                copies.send(source.at[:, :edge], ahead.at[:, width - edge :], at_phase(-1)),
            ]
            back[:, edge:] = source[:, : width - edge]
            ahead[:, : width - edge] = source[:, edge:]
            return got
        if (2 * hops) % phase_n == 0:
            return [copies.send(source, back, at_phase(hops))]
        return [
            copies.send(source, back, at_phase(hops)),
            copies.send(source, ahead, at_phase(-hops)),
        ]

    def read_neighbours(back, ahead, got):
        for copy in got:
            copy.wait_recv()
        back_values = back[...].astype(f32)
        if len(got) == 1:
            return back_values, back_values
        return back_values, ahead[...].astype(f32)

    def wait_all(got):
        for copy in got:
            copy.wait_recv()

    got_frames = spread_rows(frames, fr_x)
    got_cotangent = spread_rows(cotangent, cot_x)
    own_taps = taps[rows_of(z), :]

    def tap(block, index):
        number = 3 * block + index
        return own_taps[:, number : number + 1]

    wait_all(got_frames)
    state[0] = join_planes(fr_x)

    single = []
    for block in range(BLOCKS):
        reach = 2**block
        got = start_neighbours(state.at[block], behind_b.at[block], ahead_b.at[block], reach)
        single.append(len(got) == 1)
        here = state[block].astype(f32)
        back, ahead = read_neighbours(behind_b.at[block], ahead_b.at[block], got)
        mix = tap(block, 0) * back + tap(block, 1) * here + tap(block, 2) * ahead
        mixed[block, rows_of(z), :] = mix.astype(b16)
        got = []
        for hop in range(1, chan_n):
            part = mixed.at[block, rows_of(z), :]
            got.append(copies.send(part, part, at_chan(hop)))
        wait_all(got)
        full = mixed[block].astype(f32)
        for number, moved in enumerate(cell_shifts(full, 1)):
            stack[block, number * chans : (number + 1) * chans, :] = moved
        parts = jnp.dot(w_fwd[block], stack[block], preferred_element_type=f32)
        rows = 2 * own
        conv = (
            parts[rows : 2 * rows]
            + plane_shift(parts[:rows], -1, phase_rows)
            + plane_shift(parts[2 * rows :], 1, phase_rows)
        )
        sig = jax.nn.sigmoid(conv[own:])
        value[block] = conv[:own]
        gate[block] = sig
        state[block + 1] = (here + conv[:own] * sig).astype(b16)

    got_final = spread_planes(state[BLOCKS], final_send, final_out)

    wait_all(got_cotangent)
    grad = join_planes(cot_x).astype(f32)
    tap_lane = lax.broadcasted_iota(jnp.int32, tap_send.shape, 1)
    tap_sums = jnp.zeros(tap_send.shape, f32)
    got_final_grads = []

    def reduce_kernel(block, got):
        wait_all(got)
        total = gw_send[block, rows_chunk(p), :].astype(f32)
        for hop in range(1, phase_n):
            source = lax.rem(p + hop, phase_n)
            total = total + gw_recv[block, source].astype(f32)
        gw_out[block, p] = total.astype(b16)
        for hop in range(1, phase_n):
            part = gw_out.at[block, p]
            got_final_grads.append(copies.send(part, part, at_phase(hop)))

    def rows_chunk(index):
        return pl.ds(pl.multiple_of(index * chunk, chunk), chunk)

    waiting = None
    for block in reversed(range(BLOCKS)):
        reach = 2**block
        sig, val = gate[block], value[block]
        gz = jnp.concatenate([grad * sig, grad * val * sig * (1.0 - sig)], axis=0)
        for number, moved in enumerate(cell_shifts(gz.astype(b16).astype(f32), -1)):
            gz_stack[number * 2 * own : (number + 1) * 2 * own, :] = moved
        parts = jnp.dot(w_bwd[block], gz_stack[...], preferred_element_type=f32)
        gm = (
            parts[chans : 2 * chans]
            + plane_shift(parts[:chans], 1, phase_rows)
            + plane_shift(parts[2 * chans :], -1, phase_rows)
        )
        gm_send[block] = gm.astype(b16)
        gm_full[...] = gm
        got = []
        for hop in range(1, chan_n):
            there = at_chan(hop)
            got.append(
                copies.send(
                    gm_send.at[block, rows_of(there["chan"]), :], gm_recv.at[block, z], there
                )
            )
        low = gz.astype(b16)
        sides = jnp.concatenate(
            [plane_shift(low, 1, phase_rows), low, plane_shift(low, -1, phase_rows)], axis=0
        )
        products = lax.dot_general(
            stack[block], sides, (((1,), (1,)), ((), ())), preferred_element_type=f32
        )
        gw_send[block, : products.shape[0], :] = products.astype(b16)
        extra = gw_send.shape[1] - products.shape[0]
        if extra:
            gw_send[block, products.shape[0] :, :] = jnp.zeros((extra, products.shape[1]), b16)
        kernel_got = []
        for hop in range(1, phase_n):
            there = at_phase(hop)
            kernel_got.append(
                copies.send(
                    gw_send.at[block, rows_chunk(there["phase"]), :], gw_recv.at[block, p], there
                )
            )
        wait_all(got)
        mix_grad = gm_full[rows_of(z), :]
        for hop in range(1, chan_n):
            mix_grad = mix_grad + gm_recv[block, lax.rem(z + hop, chan_n)].astype(f32)
        gl[block] = mix_grad.astype(b16)
        got = start_neighbours(gl.at[block], gl_back.at[block], gl_ahead.at[block], reach)
        ahead_state = behind_b if single[block] else ahead_b
        for index, factor in enumerate((behind_b, state, ahead_state)):
            total = jnp.sum(mix_grad * factor[block].astype(f32), axis=1, keepdims=True)
            tap_sums = jnp.where(tap_lane == 3 * block + index, total, tap_sums)
        if waiting is not None:
            reduce_kernel(*waiting)
        waiting = (block, kernel_got)
        low = gl[block].astype(f32)
        back, ahead = read_neighbours(gl_back.at[block], gl_ahead.at[block], got)
        moved = grad + tap(block, 0) * ahead + tap(block, 1) * low + tap(block, 2) * back
        rounded = moved.astype(b16)
        grad = rounded.astype(f32)
        if block == 0:
            tap_send[...] = tap_sums
            tap_got = []
            for hop in range(1, phase_n):
                tap_got.append(copies.send(tap_send, tap_recv.at[p], at_phase(hop)))
            got_grad = spread_planes(rounded, grad_send, grad_out)

    reduce_kernel(*waiting)
    wait_all(tap_got)
    tap_recv[p] = tap_send[...]
    total = tap_recv[0]
    for index in range(1, phase_n):
        total = total + tap_recv[index]
    taps_out[z] = total
    got_taps = []
    for hop in range(1, chan_n):
        part = taps_out.at[z]
        got_taps.append(copies.send(part, part, at_chan(hop)))
    wait_all(got_final)
    wait_all(got_grad)
    wait_all(got_taps)
    wait_all(got_final_grads)
    for copy in copies.started:
        copy.wait_send()


def fused(frames, temporal_taps, conv_weights, cotangent):
    chans, phase_rows, local = frames.shape
    phase_n, chan_n = lax.axis_size("phase"), lax.axis_size("chan")
    own = chans // chan_n
    whole = local * chan_n
    width = phase_rows * whole
    flat = phase_rows * local
    stack_rows = 9 * chans
    chunk = -(-stack_rows // (16 * phase_n)) * 16
    b16, f32 = jnp.bfloat16, jnp.float32
    split = conv_weights.reshape(BLOCKS, chans, 3, 9, 2, own)
    w_fwd = jnp.transpose(split, (0, 2, 4, 5, 3, 1)).reshape(BLOCKS, 6 * own, 9 * chans)
    w_bwd = jnp.transpose(split, (0, 2, 1, 3, 4, 5)).reshape(BLOCKS, 3 * chans, 18 * own)
    taps = jnp.transpose(temporal_taps, (2, 0, 1)).reshape(chans, 3 * BLOCKS)
    count = copy_count(phase_n, chan_n, BLOCKS)
    dims = (phase_n, chan_n, phase_rows, own, whole, chunk)
    vmem = pl.BlockSpec(memory_space=pltpu.VMEM)
    final, grad, kernels, tap_sums = pl.pallas_call(
        functools.partial(fused_kernel, dims),
        out_shape=(
            jax.ShapeDtypeStruct((chan_n, own, flat), b16),
            jax.ShapeDtypeStruct((chan_n, own, flat), b16),
            jax.ShapeDtypeStruct((BLOCKS, phase_n, chunk, 6 * own), b16),
            jax.ShapeDtypeStruct((chan_n, own, 128), f32),
        ),
        in_specs=[vmem] * 5,
        out_specs=(vmem,) * 4,
        scratch_shapes=[
            pltpu.VMEM((chan_n, own, flat), b16),
            pltpu.VMEM((chan_n, own, flat), b16),
            pltpu.VMEM((BLOCKS + 1, own, width), b16),
            pltpu.VMEM((BLOCKS, own, width), b16),
            pltpu.VMEM((BLOCKS, own, width), b16),
            pltpu.VMEM((BLOCKS, chans, width), b16),
            pltpu.VMEM((BLOCKS, stack_rows, width), b16),
            pltpu.VMEM((BLOCKS, own, width), f32),
            pltpu.VMEM((BLOCKS, own, width), f32),
            pltpu.VMEM((18 * own, width), b16),
            pltpu.VMEM((BLOCKS, chans, width), b16),
            pltpu.VMEM((chans, width), f32),
            pltpu.VMEM((BLOCKS, chan_n, own, width), b16),
            pltpu.VMEM((BLOCKS, own, width), b16),
            pltpu.VMEM((BLOCKS, own, width), b16),
            pltpu.VMEM((BLOCKS, own, width), b16),
            pltpu.VMEM((BLOCKS, chunk * phase_n, 6 * own), b16),
            pltpu.VMEM((BLOCKS, phase_n, chunk, 6 * own), b16),
            pltpu.VMEM((own, 128), f32),
            pltpu.VMEM((phase_n, own, 128), f32),
            pltpu.VMEM((chan_n, own, flat), b16),
            pltpu.VMEM((chan_n, own, flat), b16),
            pltpu.SemaphoreType.DMA((count,)),
            pltpu.SemaphoreType.DMA((count,)),
        ],
        compiler_params=pltpu.CompilerParams(
            collective_id=0, has_side_effects=True, vmem_limit_bytes=48 * 1024 * 1024
        ),
        name="fused_blocks",
    )(frames.reshape(chans, flat), cotangent.reshape(chans, flat), taps, w_fwd, w_bwd)
    final = final.reshape(chans, phase_rows, local)
    grad = grad.reshape(chans, phase_rows, local)
    kernels = kernels.reshape(BLOCKS, phase_n * chunk, 6 * own)[:, :stack_rows]
    kernels = kernels.reshape(BLOCKS, 9, chans, 3, 2, own)
    kernels = jnp.transpose(kernels, (0, 2, 3, 1, 4, 5)).reshape(conv_weights.shape)
    tap_sums = tap_sums.reshape(chans, 128)[:, : 3 * BLOCKS]
    tap_sums = jnp.transpose(tap_sums).reshape(temporal_taps.shape)
    return (final, grad, tap_sums, kernels.astype(f32))


def fits(frames):
    chans, phase_rows, local = frames.shape
    phase_n, chan_n = lax.axis_size("phase"), lax.axis_size("chan")
    whole_hops = all(
        2**block < phase_rows
        or (2**block % phase_rows == 0 and (2**block // phase_rows) % phase_n != 0)
        for block in range(BLOCKS)
    )
    return (
        phase_n > 2
        and chan_n > 1
        and chans % (16 * chan_n) == 0
        and local % 128 == 0
        and SY * SZ == 128
        and whole_hops
    )


def any_size(frames, temporal_taps, conv_weights, cotangent):
    body = fused if fits(frames) else per_device
    return body(frames, temporal_taps, conv_weights, cotangent)


def solution(mesh):
    in_specs = (
        P(None, "phase", "chan"),
        P(),
        P(None, None, None, None, "chan"),
        P(None, "phase", "chan"),
    )
    out_specs = (
        P(None, "phase", "chan"),
        P(None, "phase", "chan"),
        P(),
        P(None, None, None, None, "chan"),
    )
    return jax.shard_map(
        any_size, mesh=mesh, in_specs=in_specs, out_specs=out_specs, check_vma=False
    )
```

```python
import functools

import jax
import jax.numpy as jnp
from jax import lax
from jax.experimental import pallas as pl
from jax.experimental.pallas import tpu as pltpu
from jax.sharding import PartitionSpec as P

BLOCKS = 4
SY = 8
SZ = 16


cell_offsets = [
    (kernel_pos // 9 - 1, kernel_pos // 3 % 3 - 1, kernel_pos % 3 - 1) for kernel_pos in range(27)
]


def shifted(block, axis, distance):
    devices = range(lax.axis_size(axis))
    route = [((i - distance) % len(devices), i) for i in devices]
    return lax.ppermute(block, axis, route)


def padded_2(cells, sides, width):
    for axis, dim in sides:
        count = lax.axis_size(axis)
        ends = count - 1
        head = lax.slice_in_dim(cells, 0, width, axis=dim)
        tail = lax.slice_in_dim(cells, cells.shape[dim] - width, cells.shape[dim], axis=dim)
        cells = jnp.concatenate(
            [
                lax.ppermute(tail, axis, [(i, (i + 1) % count) for i in range(ends)]),
                cells,
                lax.ppermute(head, axis, [((i + 1) % count, i) for i in range(ends)]),
            ],
            axis=dim,
        )
    return cells


def within_plane(source, step_y, step_z):
    cell_count = source.shape[-1]
    last_dim = source.ndim - 1
    margin = SZ + 1
    moved = step_y * SZ + step_z
    padded = jnp.pad(source, [(0, 0)] * last_dim + [(margin, margin)])
    window = lax.slice_in_dim(padded, margin + moved, margin + moved + cell_count, axis=last_dim)
    places = jnp.arange(cell_count, dtype=jnp.int32)
    coord_y = places // SZ + step_y
    coord_z = places % SZ + step_z
    inside = (coord_y >= 0) & (coord_y < SY) & (coord_z >= 0) & (coord_z < SZ)
    return jnp.where(inside, window, jnp.zeros_like(window))


def shifted_cells(rimmed, step_x, step_y, step_z):
    planes = rimmed.shape[-2] - 2
    rows = lax.slice_in_dim(rimmed, 1 + step_x, 1 + step_x + planes, axis=rimmed.ndim - 2)
    moved = within_plane(rows, step_y, step_z)
    return moved.reshape(moved.shape[:-2] + (planes * moved.shape[-1],))


def offset_stack(rimmed, first, count, sign):
    picked = cell_offsets[first : first + count]
    return jnp.stack(
        [
            shifted_cells(rimmed, sign * offset[0], sign * offset[1], sign * offset[2])
            for offset in picked
        ],
        axis=1,
    )


def back_block(source, hops):
    if hops == 0:
        return source
    return shifted(source, "phase", hops)


def next_block(source, hops):
    if hops == 0:
        return source
    return shifted(source, "phase", -hops)


def neighbours(source, reach):
    phase_rows = source.shape[1]
    hops, rest = divmod(reach, phase_rows)
    if rest == 0:
        return (back_block(source, hops), next_block(source, hops))
    joined = jnp.concatenate([back_block(source, hops + 1), back_block(source, hops)], axis=1)
    behind = joined[:, phase_rows - rest : 2 * phase_rows - rest]
    joined = jnp.concatenate([next_block(source, hops), next_block(source, hops + 1)], axis=1)
    ahead = joined[:, rest : rest + phase_rows]
    return (behind, ahead)


def per_device(frames, temporal_taps, conv_weights, cotangent):
    chans, phase_rows, cell_count = frames.shape
    plane_cells = SY * SZ
    planes = cell_count // plane_cells
    state = frames
    saved = []
    for block_num in range(BLOCKS):
        reach = 2**block_num
        behind, ahead = neighbours(state, reach)
        tap_rows = temporal_taps[block_num][:, :, None, None]
        mixed = (
            tap_rows[0] * behind.astype(jnp.float32)
            + tap_rows[1] * state.astype(jnp.float32)
            + tap_rows[2] * ahead.astype(jnp.float32)
        ).astype(jnp.bfloat16)
        rimmed = padded_2(mixed.reshape(chans, phase_rows, planes, plane_cells), (("chan", 2),), 1)
        kernel = lax.all_gather(conv_weights[block_num], "chan", axis=3, tiled=True)
        conv_out = jnp.zeros((chans, 2, phase_rows, cell_count), jnp.float32)
        for first in range(0, 27, 9):
            group = offset_stack(rimmed, first, 9, 1)
            conv_out = conv_out + jnp.einsum(
                "ikpv,ikgo->ogpv",
                group,
                kernel[:, first : first + 9],
                preferred_element_type=jnp.float32,
            )
        value_part = conv_out[:, 0]
        gate_sig = jax.nn.sigmoid(conv_out[:, 1])
        saved.append((state, behind, ahead, rimmed, kernel, value_part, gate_sig))
        state = (state.astype(jnp.float32) + value_part * gate_sig).astype(jnp.bfloat16)
    grad_state = cotangent
    weight_grads = [None] * BLOCKS
    tap_grads = [None] * BLOCKS
    for block_num in reversed(range(BLOCKS)):
        reach = 2**block_num
        prior, behind, ahead, rimmed, kernel, value_part, gate_sig = saved[block_num]
        tap_rows = temporal_taps[block_num][:, :, None, None]
        grad_y = grad_state.astype(jnp.float32)
        grad_z = jnp.stack(
            [grad_y * gate_sig, grad_y * value_part * gate_sig * (1.0 - gate_sig)], axis=1
        ).astype(jnp.bfloat16)
        rim_grad = padded_2(
            grad_z.reshape(chans, 2, phase_rows, planes, plane_cells), (("chan", 3),), 1
        )
        grad_mix = jnp.zeros((chans, phase_rows, cell_count), jnp.float32)
        for first in range(0, 27, 3):
            group = offset_stack(rim_grad, first, 3, -1)
            grad_mix = grad_mix + jnp.einsum(
                "okgpv,ikgo->ipv",
                group,
                kernel[:, first : first + 3],
                preferred_element_type=jnp.float32,
            )
        kernel_parts = []
        for first in range(0, 27, 9):
            group = offset_stack(rimmed, first, 9, 1)
            kernel_parts.append(
                jnp.einsum("ikpv,ogpv->ikgo", group, grad_z, preferred_element_type=jnp.float32)
            )
        grad_kernel = jnp.concatenate(kernel_parts, axis=1)
        grad_tap = jnp.stack(
            [
                jnp.sum(grad_mix * behind.astype(jnp.float32), axis=(1, 2)),
                jnp.sum(grad_mix * prior.astype(jnp.float32), axis=(1, 2)),
                jnp.sum(grad_mix * ahead.astype(jnp.float32), axis=(1, 2)),
            ]
        )
        grad_low = grad_mix.astype(jnp.bfloat16)
        back_mix, ahead_mix = neighbours(grad_low, reach)
        grad_state = (
            grad_y
            + tap_rows[0] * ahead_mix.astype(jnp.float32)
            + tap_rows[1] * grad_low.astype(jnp.float32)
            + tap_rows[2] * back_mix.astype(jnp.float32)
        ).astype(jnp.bfloat16)
        kernel_piece = lax.psum_scatter(
            grad_kernel.astype(jnp.bfloat16), "chan", scatter_dimension=3, tiled=True
        )
        grad_kernel = lax.psum(kernel_piece, "phase").astype(jnp.float32)
        weight_grads[block_num] = grad_kernel
        tap_grads[block_num] = grad_tap
    grad_weights = jnp.stack(weight_grads)
    grad_taps = lax.psum(jnp.stack(tap_grads), ("phase", "chan"))
    return (state, grad_state, grad_taps, grad_weights)


class Copies:
    def __init__(self, send_sems, recv_sems):
        self.send_sems = send_sems
        self.recv_sems = recv_sems
        self.started = []

    def send(self, src, dst, target):
        number = len(self.started)
        copy = pltpu.make_async_remote_copy(
            src_ref=src,
            dst_ref=dst,
            send_sem=self.send_sems.at[number],
            recv_sem=self.recv_sems.at[number],
            device_id=target,
            device_id_type=pl.DeviceIdType.MESH,
        )
        copy.start()
        self.started.append(copy)
        return copy


def copy_count(phase_n, chan_n, blocks):
    return (
        blocks * (2 + (chan_n - 1))
        + blocks * ((chan_n - 1) + 2 + 2 * (phase_n - 1))
        + (phase_n - 1)
        + (chan_n - 1)
    )


def plane_shift(array, step, phase_rows):
    if step == 0:
        return array
    width = array.shape[1] // phase_rows
    cells = SY * SZ
    blank = jnp.zeros((array.shape[0], cells), array.dtype)
    pieces = []
    for row in range(phase_rows):
        base = row * width
        if step < 0:
            pieces += [blank, array[:, base : base + width - cells]]
        else:
            pieces += [array[:, base + cells : base + width], blank]
    return jnp.concatenate(pieces, axis=1)


def fused_kernel(
    dims,
    frames,
    cotangent,
    taps,
    weights,
    final_out,
    grad_out,
    gw_out,
    taps_out,
    w_fwd,
    w_bwd,
    behind_v,
    ahead_v,
    gw_all,
    fr_x,
    cot_x,
    state,
    behind_b,
    ahead_b,
    mixed,
    stack,
    value,
    gate,
    gz_stack,
    gm_send,
    gm_full,
    gm_recv,
    gl,
    gl_back,
    gl_ahead,
    gw_send,
    gw_recv,
    tap_send,
    tap_recv,
    final_send,
    grad_send,
    send_sems,
    recv_sems,
    move_send,
    move_recv,
):
    phase_n, chan_n, phase_rows, own, whole, chunk = dims
    chans = own * chan_n
    width = phase_rows * whole
    local = whole // chan_n
    cells = SY * SZ
    p = lax.axis_index("phase")
    z = lax.axis_index("chan")
    copies = Copies(send_sems, recv_sems)
    f32, b16 = jnp.float32, jnp.bfloat16

    def at_phase(hop):
        return {"phase": lax.rem(p + (hop % phase_n), phase_n), "chan": z}

    def at_chan(hop):
        return {"phase": p, "chan": lax.rem(z + (hop % chan_n), chan_n)}

    def rows_of(index):
        return pl.ds(pl.multiple_of(index * own, own), own)

    half = phase_n // 2
    q = lax.rem(p, 2) * half + lax.div(p, 2)

    def holder(residue):
        return lax.rem(residue, half) * 2 + lax.div(residue, half)

    def at_residue(hop):
        return {"phase": holder(lax.rem(q + (hop % phase_n), phase_n)), "chan": z}

    everyone = phase_n * chan_n
    barrier = pltpu.get_barrier_semaphore()
    for hop in range(1, everyone):
        number = lax.rem(p * chan_n + z + hop, everyone)
        other = {"phase": lax.div(number, chan_n), "chan": lax.rem(number, chan_n)}
        pl.semaphore_signal(
            barrier, inc=1, device_id=other, device_id_type=pl.DeviceIdType.MESH
        )
    pl.semaphore_wait(barrier, everyone - 1)

    lane = lax.broadcasted_iota(jnp.int32, (1, width), 1)
    coord_z = lax.rem(lane, SZ)
    coord_y = lax.rem(lane // SZ, SY)
    steps = [(k // 3 - 1, k % 3 - 1) for k in range(9)]
    masks = {}
    for step_y, step_z in steps:
        y, w = coord_y + step_y, coord_z + step_z
        masks[step_y, step_z] = (
            ((y >= 0) & (y < SY) & (w >= 0) & (w < SZ)).astype(f32)
        )

    def cell_shifts(array, sign):
        for step_y, step_z in steps:
            step_y, step_z = sign * step_y, sign * step_z
            moved = step_y * SZ + step_z
            if moved == 0:
                yield array.astype(b16)
            else:
                rolled = pltpu.roll(array, (-moved) % width, axis=1)
                yield (rolled * masks[step_y, step_z]).astype(b16)

    moves = []

    def working_place(index):
        phase = phase_rows * p + index
        return holder(lax.rem(phase, phase_n)), lax.div(phase, phase_n)

    def home_place(index):
        phase = q + phase_n * index
        return lax.div(phase, phase_rows), lax.rem(phase, phase_rows)

    def move(group, source, target, place):
        for index in range(phase_rows):
            where, slot = place(index)
            for hop in range(chan_n):
                chan = lax.rem(z + hop, chan_n)
                src, dst = source(index, chan), target.at[slot, z]
                recv_sem = move_recv.at[group, slot * chan_n + z]
                copy = pltpu.make_async_remote_copy(
                    src_ref=src,
                    dst_ref=dst,
                    send_sem=move_send.at[group, index * chan_n + hop],
                    recv_sem=recv_sem,
                    device_id={"phase": where, "chan": chan},
                    device_id_type=pl.DeviceIdType.MESH,
                )
                if hop:
                    copy.start()
                    moves.append((copy, None))
                else:
                    pl.when(where != p)(copy.start)
                    pl.when(where == p)(pltpu.make_async_copy(src, dst, recv_sem).start)
                    moves.append((copy, where))

    def arrived(group, target):
        for slot in range(phase_rows):
            for chan in range(chan_n):
                part = target.at[slot, chan]
                pltpu.make_async_copy(
                    part, part, move_recv.at[group, slot * chan_n + chan]
                ).wait()

    def join_planes(parts):
        return jnp.concatenate(
            [parts[u, chan] for u in range(phase_rows) for chan in range(chan_n)], axis=1
        )

    def send_home(group, array, stage, target):
        for u in range(phase_rows):
            for chan in range(chan_n):
                base = u * whole + chan * local
                stage[u, chan] = array[:, base : base + local]
        move(group, lambda index, chan: stage.at[index, chan], target, home_place)

    def turned(array, count):
        cut_at = (count % phase_rows) * whole
        if cut_at == 0:
            return array
        return jnp.concatenate([array[:, width - cut_at :], array[:, : width - cut_at]], axis=1)

    def start_neighbours(source, back, ahead, reach):
        if reach % phase_n == 0:
            return []
        got = [copies.send(source, back, at_residue(reach))]
        if (2 * reach) % phase_n:
            got.append(copies.send(source, ahead, at_residue(-reach)))
        return got

    def read_neighbours(source, back, ahead, got, reach):
        if not got:
            here = source[...].astype(f32)
            return turned(here, reach // phase_n), turned(here, -(reach // phase_n))
        for copy in got:
            copy.wait_recv()
        back_raw = back[...].astype(f32)
        ahead_raw = back_raw if len(got) == 1 else ahead[...].astype(f32)
        return (
            jnp.where(q >= reach, back_raw, turned(back_raw, 1)),
            jnp.where(q + reach < phase_n, ahead_raw, turned(ahead_raw, -1)),
        )

    def wait_all(got):
        for copy in got:
            copy.wait_recv()

    move(0, lambda index, chan: frames.at[index, rows_of(chan), :], fr_x, working_place)
    move(1, lambda index, chan: cotangent.at[index, rows_of(chan), :], cot_x, working_place)
    pair = 2 * own
    for block in range(BLOCKS):
        for step in range(3):
            rows = weights[block, step * 9 * pair : (step + 1) * 9 * pair, :]
            w_fwd[block, step * pair : (step + 1) * pair, :] = jnp.concatenate(
                [rows[k * pair : (k + 1) * pair] for k in range(9)], axis=1
            )
            w_bwd[block, step * chans : (step + 1) * chans, :] = jnp.transpose(
                rows.astype(f32)
            ).astype(b16)
    own_taps = taps[rows_of(z), :]

    def tap(block, index):
        number = 3 * block + index
        return own_taps[:, number : number + 1]

    arrived(0, fr_x)
    state[0] = join_planes(fr_x)

    for block in range(BLOCKS):
        reach = 2**block
        got = start_neighbours(state.at[block], behind_b.at[block], ahead_b.at[block], reach)
        here = state[block].astype(f32)
        back, ahead = read_neighbours(
            state.at[block], behind_b.at[block], ahead_b.at[block], got, reach
        )
        behind_v[block] = back.astype(b16)
        ahead_v[block] = ahead.astype(b16)
        mix = tap(block, 0) * back + tap(block, 1) * here + tap(block, 2) * ahead
        mixed[block, rows_of(z), :] = mix.astype(b16)
        got = []
        for hop in range(1, chan_n):
            part = mixed.at[block, rows_of(z), :]
            got.append(copies.send(part, part, at_chan(hop)))
        wait_all(got)
        full = mixed[block].astype(f32)
        for number, moved in enumerate(cell_shifts(full, 1)):
            stack[block, number * chans : (number + 1) * chans, :] = moved
        parts = jnp.dot(w_fwd[block], stack[block], preferred_element_type=f32)
        rows = 2 * own
        conv = (
            parts[rows : 2 * rows]
            + plane_shift(parts[:rows], -1, phase_rows)
            + plane_shift(parts[2 * rows :], 1, phase_rows)
        )
        sig = jax.nn.sigmoid(conv[own:])
        value[block] = conv[:own]
        gate[block] = sig
        state[block + 1] = (here + conv[:own] * sig).astype(b16)

    send_home(2, state[BLOCKS], final_send, final_out)

    arrived(1, cot_x)
    grad = join_planes(cot_x).astype(f32)
    tap_lane = lax.broadcasted_iota(jnp.int32, tap_send.shape, 1)
    tap_sums = jnp.zeros(tap_send.shape, f32)
    got_final_grads = []

    def reduce_kernel(block, got):
        wait_all(got)
        total = gw_send[block, rows_chunk(p), :].astype(f32)
        for hop in range(1, phase_n):
            source = lax.rem(p + hop, phase_n)
            total = total + gw_recv[block, source].astype(f32)
        gw_all[block, p] = total.astype(b16)
        for hop in range(1, phase_n):
            part = gw_all.at[block, p]
            got_final_grads.append(copies.send(part, part, at_phase(hop)))

    def rows_chunk(index):
        return pl.ds(pl.multiple_of(index * chunk, chunk), chunk)

    waiting = None
    for block in reversed(range(BLOCKS)):
        reach = 2**block
        sig, val = gate[block], value[block]
        gz = jnp.concatenate([grad * sig, grad * val * sig * (1.0 - sig)], axis=0)
        for number, moved in enumerate(cell_shifts(gz.astype(b16).astype(f32), -1)):
            gz_stack[number * 2 * own : (number + 1) * 2 * own, :] = moved
        parts = jnp.dot(w_bwd[block], gz_stack[...], preferred_element_type=f32)
        gm = (
            parts[chans : 2 * chans]
            + plane_shift(parts[:chans], 1, phase_rows)
            + plane_shift(parts[2 * chans :], -1, phase_rows)
        )
        gm_send[block] = gm.astype(b16)
        gm_full[...] = gm
        got = []
        for hop in range(1, chan_n):
            there = at_chan(hop)
            got.append(
                copies.send(
                    gm_send.at[block, rows_of(there["chan"]), :], gm_recv.at[block, z], there
                )
            )
        low = gz.astype(b16)
        sides = jnp.concatenate(
            [plane_shift(low, 1, phase_rows), low, plane_shift(low, -1, phase_rows)], axis=0
        )
        products = lax.dot_general(
            sides, stack[block], (((1,), (1,)), ((), ())), preferred_element_type=f32
        ).astype(b16)
        wide = -(-products.shape[1] // 128) * 128
        if wide != products.shape[1]:
            blank = jnp.zeros((6 * own, wide - products.shape[1]), b16)
            products = jnp.concatenate([products, blank], axis=1)
        filled = 6 * own * (wide // 128)
        for tile in range(wide // 128):
            gw_send[block, tile * 6 * own : (tile + 1) * 6 * own, :] = products[
                :, tile * 128 : (tile + 1) * 128
            ]
        if filled < gw_send.shape[1]:
            gw_send[block, filled:, :] = jnp.zeros((gw_send.shape[1] - filled, 128), b16)
        kernel_got = []
        for hop in range(1, phase_n):
            there = at_phase(hop)
            kernel_got.append(
                copies.send(
                    gw_send.at[block, rows_chunk(there["phase"]), :], gw_recv.at[block, p], there
                )
            )
        wait_all(got)
        mix_grad = gm_full[rows_of(z), :]
        for hop in range(1, chan_n):
            mix_grad = mix_grad + gm_recv[block, lax.rem(z + hop, chan_n)].astype(f32)
        gl[block] = mix_grad.astype(b16)
        got = start_neighbours(gl.at[block], gl_back.at[block], gl_ahead.at[block], reach)
        for index, factor in enumerate((behind_v, state, ahead_v)):
            total = jnp.sum(mix_grad * factor[block].astype(f32), axis=1, keepdims=True)
            tap_sums = jnp.where(tap_lane == 3 * block + index, total, tap_sums)
        if waiting is not None:
            reduce_kernel(*waiting)
        waiting = (block, kernel_got)
        low = gl[block].astype(f32)
        back, ahead = read_neighbours(
            gl.at[block], gl_back.at[block], gl_ahead.at[block], got, reach
        )
        moved = grad + tap(block, 0) * ahead + tap(block, 1) * low + tap(block, 2) * back
        rounded = moved.astype(b16)
        grad = rounded.astype(f32)
        if block == 0:
            tap_send[...] = tap_sums
            tap_got = []
            for hop in range(1, phase_n):
                tap_got.append(copies.send(tap_send, tap_recv.at[p], at_phase(hop)))
            send_home(3, rounded, grad_send, grad_out)

    reduce_kernel(*waiting)
    wait_all(tap_got)
    tap_recv[p] = tap_send[...]
    total = tap_recv[0]
    for index in range(1, phase_n):
        total = total + tap_recv[index]
    taps_out[z] = total
    got_taps = []
    for hop in range(1, chan_n):
        part = taps_out.at[z]
        got_taps.append(copies.send(part, part, at_chan(hop)))
    wait_all(got_final_grads)
    per_tile = 128 // chans
    for block in range(BLOCKS):
        joined = jnp.concatenate([gw_all[block, index] for index in range(phase_n)], axis=0)
        for step in range(3):
            for k in range(9):
                top = (k // per_tile) * 6 * own + step * pair
                left = (k % per_tile) * chans
                base = (step * 9 + k) * pair
                gw_out[block, base : base + pair, :] = joined[
                    top : top + pair, left : left + chans
                ]
    arrived(2, final_out)
    arrived(3, grad_out)
    wait_all(got_taps)
    for copy, where in moves:
        if where is None:
            copy.wait_send()
        else:
            pl.when(where != p)(copy.wait_send)
    for copy in copies.started:
        copy.wait_send()


def fused(frames, temporal_taps, conv_weights, cotangent):
    chans, phase_rows, local = frames.shape
    phase_n, chan_n = lax.axis_size("phase"), lax.axis_size("chan")
    own = chans // chan_n
    whole = local * chan_n
    width = phase_rows * whole
    stack_rows = 9 * chans
    kernel_rows = 6 * own * -(-stack_rows // 128)
    chunk = -(-kernel_rows // (16 * phase_n)) * 16
    b16, f32 = jnp.bfloat16, jnp.float32
    weights = jnp.transpose(conv_weights, (0, 2, 3, 4, 1)).reshape(BLOCKS, 54 * own, chans)
    taps = jnp.transpose(temporal_taps, (2, 0, 1)).reshape(chans, 3 * BLOCKS)
    count = copy_count(phase_n, chan_n, BLOCKS)
    dims = (phase_n, chan_n, phase_rows, own, whole, chunk)
    vmem = pl.BlockSpec(memory_space=pltpu.VMEM)
    final, grad, kernels, tap_sums = pl.pallas_call(
        functools.partial(fused_kernel, dims),
        out_shape=(
            jax.ShapeDtypeStruct((phase_rows, chan_n, own, local), b16),
            jax.ShapeDtypeStruct((phase_rows, chan_n, own, local), b16),
            jax.ShapeDtypeStruct((BLOCKS, 54 * own, chans), b16),
            jax.ShapeDtypeStruct((chan_n, own, 128), f32),
        ),
        in_specs=[vmem] * 4,
        out_specs=(vmem,) * 4,
        scratch_shapes=[
            pltpu.VMEM((BLOCKS, 6 * own, 9 * chans), b16),
            pltpu.VMEM((BLOCKS, 3 * chans, 18 * own), b16),
            pltpu.VMEM((BLOCKS, own, width), b16),
            pltpu.VMEM((BLOCKS, own, width), b16),
            pltpu.VMEM((BLOCKS, phase_n, chunk, 128), b16),
            pltpu.VMEM((phase_rows, chan_n, own, local), b16),
            pltpu.VMEM((phase_rows, chan_n, own, local), b16),
            pltpu.VMEM((BLOCKS + 1, own, width), b16),
            pltpu.VMEM((BLOCKS, own, width), b16),
            pltpu.VMEM((BLOCKS, own, width), b16),
            pltpu.VMEM((BLOCKS, chans, width), b16),
            pltpu.VMEM((BLOCKS, stack_rows, width), b16),
            pltpu.VMEM((BLOCKS, own, width), f32),
            pltpu.VMEM((BLOCKS, own, width), f32),
            pltpu.VMEM((18 * own, width), b16),
            pltpu.VMEM((BLOCKS, chans, width), b16),
            pltpu.VMEM((chans, width), f32),
            pltpu.VMEM((BLOCKS, chan_n, own, width), b16),
            pltpu.VMEM((BLOCKS, own, width), b16),
            pltpu.VMEM((BLOCKS, own, width), b16),
            pltpu.VMEM((BLOCKS, own, width), b16),
            pltpu.VMEM((BLOCKS, chunk * phase_n, 128), b16),
            pltpu.VMEM((BLOCKS, phase_n, chunk, 128), b16),
            pltpu.VMEM((own, 128), f32),
            pltpu.VMEM((phase_n, own, 128), f32),
            pltpu.VMEM((phase_rows, chan_n, own, local), b16),
            pltpu.VMEM((phase_rows, chan_n, own, local), b16),
            pltpu.SemaphoreType.DMA((count,)),
            pltpu.SemaphoreType.DMA((count,)),
            pltpu.SemaphoreType.DMA((4, phase_rows * chan_n)),
            pltpu.SemaphoreType.DMA((4, phase_rows * chan_n)),
        ],
        compiler_params=pltpu.CompilerParams(
            collective_id=0, has_side_effects=True, vmem_limit_bytes=48 * 1024 * 1024
        ),
        name="fused_blocks",
    )(jnp.swapaxes(frames, 0, 1), jnp.swapaxes(cotangent, 0, 1), taps, weights)
    final = jnp.swapaxes(final.reshape(phase_rows, chans, local), 0, 1)
    grad = jnp.swapaxes(grad.reshape(phase_rows, chans, local), 0, 1)
    kernels = jnp.transpose(kernels.reshape(BLOCKS, 27, 2, own, chans), (0, 4, 1, 2, 3))
    tap_sums = tap_sums.reshape(chans, 128)[:, : 3 * BLOCKS]
    tap_sums = jnp.transpose(tap_sums).reshape(temporal_taps.shape)
    return (final, grad, tap_sums, kernels.astype(f32))


def fits(frames):
    chans, phase_rows, local = frames.shape
    phase_n, chan_n = lax.axis_size("phase"), lax.axis_size("chan")
    whole_hops = all(
        2**block < phase_n or 2**block % phase_n == 0 for block in range(BLOCKS)
    )
    return (
        phase_n % 2 == 0
        and phase_n > 2
        and 128 % chans == 0
        and chan_n > 1
        and chans % (16 * chan_n) == 0
        and local % 128 == 0
        and SY * SZ == 128
        and whole_hops
    )


def any_size(frames, temporal_taps, conv_weights, cotangent):
    body = fused if fits(frames) else per_device
    return body(frames, temporal_taps, conv_weights, cotangent)


def solution(mesh):
    in_specs = (
        P(None, "phase", "chan"),
        P(),
        P(None, None, None, None, "chan"),
        P(None, "phase", "chan"),
    )
    out_specs = (
        P(None, "phase", "chan"),
        P(None, "phase", "chan"),
        P(),
        P(None, None, None, None, "chan"),
    )
    return jax.shard_map(
        any_size, mesh=mesh, in_specs=in_specs, out_specs=out_specs, check_vma=False
    )
```

```python
import functools

import jax
import jax.numpy as jnp
from jax import lax
from jax.experimental import pallas as pl
from jax.experimental.pallas import tpu as pltpu
from jax.sharding import PartitionSpec as P

BLOCKS = 4
SY = 8
SZ = 16


cell_offsets = [
    (kernel_pos // 9 - 1, kernel_pos // 3 % 3 - 1, kernel_pos % 3 - 1) for kernel_pos in range(27)
]


def shifted(block, axis, distance):
    devices = range(lax.axis_size(axis))
    route = [((i - distance) % len(devices), i) for i in devices]
    return lax.ppermute(block, axis, route)


def padded_2(cells, sides, width):
    for axis, dim in sides:
        count = lax.axis_size(axis)
        ends = count - 1
        head = lax.slice_in_dim(cells, 0, width, axis=dim)
        tail = lax.slice_in_dim(cells, cells.shape[dim] - width, cells.shape[dim], axis=dim)
        cells = jnp.concatenate(
            [
                lax.ppermute(tail, axis, [(i, (i + 1) % count) for i in range(ends)]),
                cells,
                lax.ppermute(head, axis, [((i + 1) % count, i) for i in range(ends)]),
            ],
            axis=dim,
        )
    return cells


def within_plane(source, step_y, step_z):
    cell_count = source.shape[-1]
    last_dim = source.ndim - 1
    margin = SZ + 1
    moved = step_y * SZ + step_z
    padded = jnp.pad(source, [(0, 0)] * last_dim + [(margin, margin)])
    window = lax.slice_in_dim(padded, margin + moved, margin + moved + cell_count, axis=last_dim)
    places = jnp.arange(cell_count, dtype=jnp.int32)
    coord_y = places // SZ + step_y
    coord_z = places % SZ + step_z
    inside = (coord_y >= 0) & (coord_y < SY) & (coord_z >= 0) & (coord_z < SZ)
    return jnp.where(inside, window, jnp.zeros_like(window))


def shifted_cells(rimmed, step_x, step_y, step_z):
    planes = rimmed.shape[-2] - 2
    rows = lax.slice_in_dim(rimmed, 1 + step_x, 1 + step_x + planes, axis=rimmed.ndim - 2)
    moved = within_plane(rows, step_y, step_z)
    return moved.reshape(moved.shape[:-2] + (planes * moved.shape[-1],))


def offset_stack(rimmed, first, count, sign):
    picked = cell_offsets[first : first + count]
    return jnp.stack(
        [
            shifted_cells(rimmed, sign * offset[0], sign * offset[1], sign * offset[2])
            for offset in picked
        ],
        axis=1,
    )


def back_block(source, hops):
    if hops == 0:
        return source
    return shifted(source, "phase", hops)


def next_block(source, hops):
    if hops == 0:
        return source
    return shifted(source, "phase", -hops)


def neighbours(source, reach):
    phase_rows = source.shape[1]
    hops, rest = divmod(reach, phase_rows)
    if rest == 0:
        return (back_block(source, hops), next_block(source, hops))
    joined = jnp.concatenate([back_block(source, hops + 1), back_block(source, hops)], axis=1)
    behind = joined[:, phase_rows - rest : 2 * phase_rows - rest]
    joined = jnp.concatenate([next_block(source, hops), next_block(source, hops + 1)], axis=1)
    ahead = joined[:, rest : rest + phase_rows]
    return (behind, ahead)


def per_device(frames, temporal_taps, conv_weights, cotangent):
    chans, phase_rows, cell_count = frames.shape
    plane_cells = SY * SZ
    planes = cell_count // plane_cells
    state = frames
    saved = []
    for block_num in range(BLOCKS):
        reach = 2**block_num
        behind, ahead = neighbours(state, reach)
        tap_rows = temporal_taps[block_num][:, :, None, None]
        mixed = (
            tap_rows[0] * behind.astype(jnp.float32)
            + tap_rows[1] * state.astype(jnp.float32)
            + tap_rows[2] * ahead.astype(jnp.float32)
        ).astype(jnp.bfloat16)
        rimmed = padded_2(mixed.reshape(chans, phase_rows, planes, plane_cells), (("chan", 2),), 1)
        kernel = lax.all_gather(conv_weights[block_num], "chan", axis=3, tiled=True)
        conv_out = jnp.zeros((chans, 2, phase_rows, cell_count), jnp.float32)
        for first in range(0, 27, 9):
            group = offset_stack(rimmed, first, 9, 1)
            conv_out = conv_out + jnp.einsum(
                "ikpv,ikgo->ogpv",
                group,
                kernel[:, first : first + 9],
                preferred_element_type=jnp.float32,
            )
        value_part = conv_out[:, 0]
        gate_sig = jax.nn.sigmoid(conv_out[:, 1])
        saved.append((state, behind, ahead, rimmed, kernel, value_part, gate_sig))
        state = (state.astype(jnp.float32) + value_part * gate_sig).astype(jnp.bfloat16)
    grad_state = cotangent
    weight_grads = [None] * BLOCKS
    tap_grads = [None] * BLOCKS
    for block_num in reversed(range(BLOCKS)):
        reach = 2**block_num
        prior, behind, ahead, rimmed, kernel, value_part, gate_sig = saved[block_num]
        tap_rows = temporal_taps[block_num][:, :, None, None]
        grad_y = grad_state.astype(jnp.float32)
        grad_z = jnp.stack(
            [grad_y * gate_sig, grad_y * value_part * gate_sig * (1.0 - gate_sig)], axis=1
        ).astype(jnp.bfloat16)
        rim_grad = padded_2(
            grad_z.reshape(chans, 2, phase_rows, planes, plane_cells), (("chan", 3),), 1
        )
        grad_mix = jnp.zeros((chans, phase_rows, cell_count), jnp.float32)
        for first in range(0, 27, 3):
            group = offset_stack(rim_grad, first, 3, -1)
            grad_mix = grad_mix + jnp.einsum(
                "okgpv,ikgo->ipv",
                group,
                kernel[:, first : first + 3],
                preferred_element_type=jnp.float32,
            )
        kernel_parts = []
        for first in range(0, 27, 9):
            group = offset_stack(rimmed, first, 9, 1)
            kernel_parts.append(
                jnp.einsum("ikpv,ogpv->ikgo", group, grad_z, preferred_element_type=jnp.float32)
            )
        grad_kernel = jnp.concatenate(kernel_parts, axis=1)
        grad_tap = jnp.stack(
            [
                jnp.sum(grad_mix * behind.astype(jnp.float32), axis=(1, 2)),
                jnp.sum(grad_mix * prior.astype(jnp.float32), axis=(1, 2)),
                jnp.sum(grad_mix * ahead.astype(jnp.float32), axis=(1, 2)),
            ]
        )
        grad_low = grad_mix.astype(jnp.bfloat16)
        back_mix, ahead_mix = neighbours(grad_low, reach)
        grad_state = (
            grad_y
            + tap_rows[0] * ahead_mix.astype(jnp.float32)
            + tap_rows[1] * grad_low.astype(jnp.float32)
            + tap_rows[2] * back_mix.astype(jnp.float32)
        ).astype(jnp.bfloat16)
        kernel_piece = lax.psum_scatter(
            grad_kernel.astype(jnp.bfloat16), "chan", scatter_dimension=3, tiled=True
        )
        grad_kernel = lax.psum(kernel_piece, "phase").astype(jnp.float32)
        weight_grads[block_num] = grad_kernel
        tap_grads[block_num] = grad_tap
    grad_weights = jnp.stack(weight_grads)
    grad_taps = lax.psum(jnp.stack(tap_grads), ("phase", "chan"))
    return (state, grad_state, grad_taps, grad_weights)


class Copies:
    def __init__(self, send_sems, recv_sems):
        self.send_sems = send_sems
        self.recv_sems = recv_sems
        self.started = []

    def send(self, src, dst, target):
        number = len(self.started)
        copy = pltpu.make_async_remote_copy(
            src_ref=src,
            dst_ref=dst,
            send_sem=self.send_sems.at[number],
            recv_sem=self.recv_sems.at[number],
            device_id=target,
            device_id_type=pl.DeviceIdType.MESH,
        )
        copy.start()
        self.started.append(copy)
        return copy


def copy_count(phase_n, chan_n, blocks):
    return (
        blocks * (2 + (chan_n - 1))
        + blocks * ((chan_n - 1) + 2 + 2 * (phase_n - 1))
        + (phase_n - 1)
        + (chan_n - 1)
    )


def plane_shift(array, step, phase_rows):
    if step == 0:
        return array
    width = array.shape[1] // phase_rows
    cells = SY * SZ
    blank = jnp.zeros((array.shape[0], cells), array.dtype)
    pieces = []
    for row in range(phase_rows):
        base = row * width
        if step < 0:
            pieces += [blank, array[:, base : base + width - cells]]
        else:
            pieces += [array[:, base + cells : base + width], blank]
    return jnp.concatenate(pieces, axis=1)


def fused_kernel(
    dims,
    frames,
    cotangent,
    taps,
    weights,
    final_out,
    grad_out,
    gw_out,
    taps_out,
    w_fwd,
    w_bwd,
    behind_v,
    ahead_v,
    gw_all,
    fr_behind,
    fr_ahead,
    home_grad,
    home_gl,
    gl_stage,
    fr_x,
    cot_x,
    state,
    behind_b,
    ahead_b,
    mixed,
    stack,
    value,
    gate,
    gz_stack,
    gm_send,
    gm_full,
    gm_recv,
    gl,
    gl_back,
    gl_ahead,
    gw_send,
    gw_recv,
    tap_send,
    tap_recv,
    final_send,
    grad_send,
    send_sems,
    recv_sems,
    move_send,
    move_recv,
):
    phase_n, chan_n, phase_rows, own, whole, chunk = dims
    chans = own * chan_n
    width = phase_rows * whole
    local = whole // chan_n
    cells = SY * SZ
    p = lax.axis_index("phase")
    z = lax.axis_index("chan")
    copies = Copies(send_sems, recv_sems)
    f32, b16 = jnp.float32, jnp.bfloat16

    def at_phase(hop):
        return {"phase": lax.rem(p + (hop % phase_n), phase_n), "chan": z}

    def at_chan(hop):
        return {"phase": p, "chan": lax.rem(z + (hop % chan_n), chan_n)}

    def rows_of(index):
        return pl.ds(pl.multiple_of(index * own, own), own)

    half = phase_n // 2
    q = lax.rem(p, 2) * half + lax.div(p, 2)

    def holder(residue):
        return lax.rem(residue, half) * 2 + lax.div(residue, half)

    def at_residue(hop):
        return {"phase": holder(lax.rem(q + (hop % phase_n), phase_n)), "chan": z}

    everyone = phase_n * chan_n
    barrier = pltpu.get_barrier_semaphore()
    for hop in range(1, everyone):
        number = lax.rem(p * chan_n + z + hop, everyone)
        other = {"phase": lax.div(number, chan_n), "chan": lax.rem(number, chan_n)}
        pl.semaphore_signal(
            barrier, inc=1, device_id=other, device_id_type=pl.DeviceIdType.MESH
        )
    pl.semaphore_wait(barrier, everyone - 1)

    lane = lax.broadcasted_iota(jnp.int32, (1, width), 1)
    coord_z = lax.rem(lane, SZ)
    coord_y = lax.rem(lane // SZ, SY)
    steps = [(k // 3 - 1, k % 3 - 1) for k in range(9)]
    masks = {}
    for step_y, step_z in steps:
        y, w = coord_y + step_y, coord_z + step_z
        masks[step_y, step_z] = (
            ((y >= 0) & (y < SY) & (w >= 0) & (w < SZ)).astype(f32)
        )

    def cell_shifts(array, sign):
        for step_y, step_z in steps:
            step_y, step_z = sign * step_y, sign * step_z
            moved = step_y * SZ + step_z
            if moved == 0:
                yield array.astype(b16)
            else:
                rolled = pltpu.roll(array, (-moved) % width, axis=1)
                yield (rolled * masks[step_y, step_z]).astype(b16)

    moves = []

    phases = phase_n * phase_rows

    def working_place(index, ahead=0):
        phase = lax.rem(phase_rows * p + index + (ahead % phases), phases)
        return holder(lax.rem(phase, phase_n)), lax.div(phase, phase_n)

    def home_place(index, ahead=0):
        phase = lax.rem(q + phase_n * index + (ahead % phases), phases)
        return lax.div(phase, phase_rows), lax.rem(phase, phase_rows)

    def move(group, source, target, place):
        for index in range(phase_rows):
            where, slot = place(index)
            for hop in range(chan_n):
                chan = lax.rem(z + hop, chan_n)
                src, dst = source(index, chan), target.at[slot, z]
                recv_sem = move_recv.at[group, slot * chan_n + z]
                copy = pltpu.make_async_remote_copy(
                    src_ref=src,
                    dst_ref=dst,
                    send_sem=move_send.at[group, index * chan_n + hop],
                    recv_sem=recv_sem,
                    device_id={"phase": where, "chan": chan},
                    device_id_type=pl.DeviceIdType.MESH,
                )
                if hop:
                    copy.start()
                    moves.append((copy, None))
                else:
                    pl.when(where != p)(copy.start)
                    pl.when(where == p)(pltpu.make_async_copy(src, dst, recv_sem).start)
                    moves.append((copy, where))

    def arrived(group, target):
        for slot in range(phase_rows):
            for chan in range(chan_n):
                part = target.at[slot, chan]
                pltpu.make_async_copy(
                    part, part, move_recv.at[group, slot * chan_n + chan]
                ).wait()

    def join_planes(parts):
        return jnp.concatenate(
            [parts[u, chan] for u in range(phase_rows) for chan in range(chan_n)], axis=1
        )

    def send_home(group, array, stage, target):
        for u in range(phase_rows):
            for chan in range(chan_n):
                base = u * whole + chan * local
                stage[u, chan] = array[:, base : base + local]
        move(group, lambda index, chan: stage.at[index, chan], target, home_place)

    def turned(array, count):
        cut_at = (count % phase_rows) * whole
        if cut_at == 0:
            return array
        return jnp.concatenate([array[:, width - cut_at :], array[:, : width - cut_at]], axis=1)

    def start_neighbours(source, back, ahead, reach):
        if reach % phase_n == 0:
            return []
        got = [copies.send(source, back, at_residue(reach))]
        if (2 * reach) % phase_n:
            got.append(copies.send(source, ahead, at_residue(-reach)))
        return got

    def read_neighbours(source, back, ahead, got, reach):
        if not got:
            here = source[...].astype(f32)
            return turned(here, reach // phase_n), turned(here, -(reach // phase_n))
        for copy in got:
            copy.wait_recv()
        back_raw = back[...].astype(f32)
        ahead_raw = back_raw if len(got) == 1 else ahead[...].astype(f32)
        return (
            jnp.where(q >= reach, back_raw, turned(back_raw, 1)),
            jnp.where(q + reach < phase_n, ahead_raw, turned(ahead_raw, -1)),
        )

    def wait_all(got):
        for copy in got:
            copy.wait_recv()

    def own_rows(source):
        return lambda index, chan: source.at[index, rows_of(chan), :]

    move(0, own_rows(frames), fr_x, working_place)
    move(4, own_rows(frames), fr_behind, functools.partial(working_place, ahead=1))
    move(5, own_rows(frames), fr_ahead, functools.partial(working_place, ahead=-1))
    pair = 2 * own
    for block in range(BLOCKS):
        for step in range(3):
            rows = weights[block, step * 9 * pair : (step + 1) * 9 * pair, :]
            w_fwd[block, step * pair : (step + 1) * pair, :] = jnp.concatenate(
                [rows[k * pair : (k + 1) * pair] for k in range(9)], axis=1
            )
            w_bwd[block, step * chans : (step + 1) * chans, :] = jnp.transpose(
                rows.astype(f32)
            ).astype(b16)
    own_taps = taps[rows_of(z), :]

    def tap(block, index):
        number = 3 * block + index
        return own_taps[:, number : number + 1]

    arrived(0, fr_x)
    state[0] = join_planes(fr_x)

    for block in range(BLOCKS):
        reach = 2**block
        here = state[block].astype(f32)
        if block == 0:
            arrived(4, fr_behind)
            arrived(5, fr_ahead)
            back = join_planes(fr_behind).astype(f32)
            ahead = join_planes(fr_ahead).astype(f32)
        else:
            got = start_neighbours(
                state.at[block], behind_b.at[block], ahead_b.at[block], reach
            )
            back, ahead = read_neighbours(
                state.at[block], behind_b.at[block], ahead_b.at[block], got, reach
            )
        behind_v[block] = back.astype(b16)
        ahead_v[block] = ahead.astype(b16)
        mix = tap(block, 0) * back + tap(block, 1) * here + tap(block, 2) * ahead
        mixed[block, rows_of(z), :] = mix.astype(b16)
        got = []
        for hop in range(1, chan_n):
            part = mixed.at[block, rows_of(z), :]
            got.append(copies.send(part, part, at_chan(hop)))
        if block == 0:
            move(1, own_rows(cotangent), cot_x, working_place)
        wait_all(got)
        full = mixed[block].astype(f32)
        for number, moved in enumerate(cell_shifts(full, 1)):
            stack[block, number * chans : (number + 1) * chans, :] = moved
        parts = jnp.dot(w_fwd[block], stack[block], preferred_element_type=f32)
        rows = 2 * own
        conv = (
            parts[rows : 2 * rows]
            + plane_shift(parts[:rows], -1, phase_rows)
            + plane_shift(parts[2 * rows :], 1, phase_rows)
        )
        sig = jax.nn.sigmoid(conv[own:])
        value[block] = conv[:own]
        gate[block] = sig
        state[block + 1] = (here + conv[:own] * sig).astype(b16)

    send_home(2, state[BLOCKS], final_send, final_out)

    arrived(1, cot_x)
    grad = join_planes(cot_x).astype(f32)
    tap_lane = lax.broadcasted_iota(jnp.int32, tap_send.shape, 1)
    tap_sums = jnp.zeros(tap_send.shape, f32)
    got_final_grads = []

    def reduce_kernel(block, got):
        wait_all(got)
        total = gw_send[block, rows_chunk(p), :].astype(f32)
        for hop in range(1, phase_n):
            source = lax.rem(p + hop, phase_n)
            total = total + gw_recv[block, source].astype(f32)
        gw_all[block, p] = total.astype(b16)
        for hop in range(1, phase_n):
            part = gw_all.at[block, p]
            got_final_grads.append(copies.send(part, part, at_phase(hop)))

    def rows_chunk(index):
        return pl.ds(pl.multiple_of(index * chunk, chunk), chunk)

    waiting = None
    for block in reversed(range(BLOCKS)):
        reach = 2**block
        sig, val = gate[block], value[block]
        gz = jnp.concatenate([grad * sig, grad * val * sig * (1.0 - sig)], axis=0)
        for number, moved in enumerate(cell_shifts(gz.astype(b16).astype(f32), -1)):
            gz_stack[number * 2 * own : (number + 1) * 2 * own, :] = moved
        parts = jnp.dot(w_bwd[block], gz_stack[...], preferred_element_type=f32)
        gm = (
            parts[chans : 2 * chans]
            + plane_shift(parts[:chans], 1, phase_rows)
            + plane_shift(parts[2 * chans :], -1, phase_rows)
        )
        gm_send[block] = gm.astype(b16)
        gm_full[...] = gm
        got = []
        for hop in range(1, chan_n):
            there = at_chan(hop)
            got.append(
                copies.send(
                    gm_send.at[block, rows_of(there["chan"]), :], gm_recv.at[block, z], there
                )
            )
        low = gz.astype(b16)
        sides = jnp.concatenate(
            [plane_shift(low, 1, phase_rows), low, plane_shift(low, -1, phase_rows)], axis=0
        )
        products = lax.dot_general(
            sides, stack[block], (((1,), (1,)), ((), ())), preferred_element_type=f32
        ).astype(b16)
        wide = -(-products.shape[1] // 128) * 128
        if wide != products.shape[1]:
            blank = jnp.zeros((6 * own, wide - products.shape[1]), b16)
            products = jnp.concatenate([products, blank], axis=1)
        filled = 6 * own * (wide // 128)
        for tile in range(wide // 128):
            gw_send[block, tile * 6 * own : (tile + 1) * 6 * own, :] = products[
                :, tile * 128 : (tile + 1) * 128
            ]
        if filled < gw_send.shape[1]:
            gw_send[block, filled:, :] = jnp.zeros((gw_send.shape[1] - filled, 128), b16)
        kernel_got = []
        for hop in range(1, phase_n):
            there = at_phase(hop)
            kernel_got.append(
                copies.send(
                    gw_send.at[block, rows_chunk(there["phase"]), :], gw_recv.at[block, p], there
                )
            )
        if waiting is not None:
            reduce_kernel(*waiting)
        waiting = (block, kernel_got)
        wait_all(got)
        mix_grad = gm_full[rows_of(z), :]
        for hop in range(1, chan_n):
            mix_grad = mix_grad + gm_recv[block, lax.rem(z + hop, chan_n)].astype(f32)
        gl[block] = mix_grad.astype(b16)
        if block == 0:
            for u in range(phase_rows):
                for chan in range(chan_n):
                    base = u * whole + chan * local
                    gl_stage[u, chan] = gl[0, :, base : base + local]
            for turn, ahead in enumerate((0, 1, -1)):
                move(
                    6 + turn,
                    lambda index, chan: gl_stage.at[index, chan],
                    home_gl.at[turn],
                    functools.partial(home_place, ahead=ahead),
                )
        else:
            got = start_neighbours(gl.at[block], gl_back.at[block], gl_ahead.at[block], reach)
        for index, factor in enumerate((behind_v, state, ahead_v)):
            total = jnp.sum(mix_grad * factor[block].astype(f32), axis=1, keepdims=True)
            tap_sums = jnp.where(tap_lane == 3 * block + index, total, tap_sums)
        if block == 0:
            tap_send[...] = tap_sums
            tap_got = []
            for hop in range(1, phase_n):
                tap_got.append(copies.send(tap_send, tap_recv.at[p], at_phase(hop)))
            break
        low = gl[block].astype(f32)
        back, ahead = read_neighbours(
            gl.at[block], gl_back.at[block], gl_ahead.at[block], got, reach
        )
        moved = grad + tap(block, 0) * ahead + tap(block, 1) * low + tap(block, 2) * back
        rounded = moved.astype(b16)
        grad = rounded.astype(f32)
        if block == 1:
            send_home(3, rounded, grad_send, home_grad)

    per_tile = 128 // chans

    def give_kernel(block):
        joined = jnp.concatenate([gw_all[block, index] for index in range(phase_n)], axis=0)
        for step in range(3):
            for k in range(9):
                top = (k // per_tile) * 6 * own + step * pair
                left = (k % per_tile) * chans
                base = (step * 9 + k) * pair
                gw_out[block, base : base + pair, :] = joined[
                    top : top + pair, left : left + chans
                ]

    reduce_kernel(*waiting)
    wait_all(got_final_grads[: 2 * (phase_n - 1)])
    for block in reversed(range(BLOCKS - 2, BLOCKS)):
        give_kernel(block)
    wait_all(tap_got)
    tap_recv[p] = tap_send[...]
    total = tap_recv[0]
    for index in range(1, phase_n):
        total = total + tap_recv[index]
    taps_out[z] = total
    got_taps = []
    for hop in range(1, chan_n):
        part = taps_out.at[z]
        got_taps.append(copies.send(part, part, at_chan(hop)))
    arrived(3, home_grad)
    for turn in range(3):
        arrived(6 + turn, home_gl.at[turn])
    for index in range(chan_n):
        columns = taps[index * own : (index + 1) * own, :]
        for slot in range(phase_rows):
            moved = (
                home_grad[slot, index].astype(f32)
                + columns[:, 0:1] * home_gl[2, slot, index].astype(f32)
                + columns[:, 1:2] * home_gl[0, slot, index].astype(f32)
                + columns[:, 2:3] * home_gl[1, slot, index].astype(f32)
            )
            grad_out[slot, index] = moved.astype(b16)
    wait_all(got_final_grads[2 * (phase_n - 1) :])
    for block in reversed(range(BLOCKS - 2)):
        give_kernel(block)
    arrived(2, final_out)
    wait_all(got_taps)
    for copy, where in moves:
        if where is None:
            copy.wait_send()
        else:
            pl.when(where != p)(copy.wait_send)
    for copy in copies.started:
        copy.wait_send()


def fused(frames, temporal_taps, conv_weights, cotangent):
    chans, phase_rows, local = frames.shape
    phase_n, chan_n = lax.axis_size("phase"), lax.axis_size("chan")
    own = chans // chan_n
    whole = local * chan_n
    width = phase_rows * whole
    stack_rows = 9 * chans
    kernel_rows = 6 * own * -(-stack_rows // 128)
    chunk = -(-kernel_rows // (16 * phase_n)) * 16
    b16, f32 = jnp.bfloat16, jnp.float32
    weights = jnp.transpose(conv_weights, (0, 2, 3, 4, 1)).reshape(BLOCKS, 54 * own, chans)
    taps = jnp.transpose(temporal_taps, (2, 0, 1)).reshape(chans, 3 * BLOCKS)
    count = copy_count(phase_n, chan_n, BLOCKS)
    dims = (phase_n, chan_n, phase_rows, own, whole, chunk)
    vmem = pl.BlockSpec(memory_space=pltpu.VMEM)
    final, grad, kernels, tap_sums = pl.pallas_call(
        functools.partial(fused_kernel, dims),
        out_shape=(
            jax.ShapeDtypeStruct((phase_rows, chan_n, own, local), b16),
            jax.ShapeDtypeStruct((phase_rows, chan_n, own, local), b16),
            jax.ShapeDtypeStruct((BLOCKS, 54 * own, chans), b16),
            jax.ShapeDtypeStruct((chan_n, own, 128), f32),
        ),
        in_specs=[vmem] * 4,
        out_specs=(vmem,) * 4,
        scratch_shapes=[
            pltpu.VMEM((BLOCKS, 6 * own, 9 * chans), b16),
            pltpu.VMEM((BLOCKS, 3 * chans, 18 * own), b16),
            pltpu.VMEM((BLOCKS, own, width), b16),
            pltpu.VMEM((BLOCKS, own, width), b16),
            pltpu.VMEM((BLOCKS, phase_n, chunk, 128), b16),
            pltpu.VMEM((phase_rows, chan_n, own, local), b16),
            pltpu.VMEM((phase_rows, chan_n, own, local), b16),
            pltpu.VMEM((phase_rows, chan_n, own, local), b16),
            pltpu.VMEM((3, phase_rows, chan_n, own, local), b16),
            pltpu.VMEM((phase_rows, chan_n, own, local), b16),
            pltpu.VMEM((phase_rows, chan_n, own, local), b16),
            pltpu.VMEM((phase_rows, chan_n, own, local), b16),
            pltpu.VMEM((BLOCKS + 1, own, width), b16),
            pltpu.VMEM((BLOCKS, own, width), b16),
            pltpu.VMEM((BLOCKS, own, width), b16),
            pltpu.VMEM((BLOCKS, chans, width), b16),
            pltpu.VMEM((BLOCKS, stack_rows, width), b16),
            pltpu.VMEM((BLOCKS, own, width), f32),
            pltpu.VMEM((BLOCKS, own, width), f32),
            pltpu.VMEM((18 * own, width), b16),
            pltpu.VMEM((BLOCKS, chans, width), b16),
            pltpu.VMEM((chans, width), f32),
            pltpu.VMEM((BLOCKS, chan_n, own, width), b16),
            pltpu.VMEM((BLOCKS, own, width), b16),
            pltpu.VMEM((BLOCKS, own, width), b16),
            pltpu.VMEM((BLOCKS, own, width), b16),
            pltpu.VMEM((BLOCKS, chunk * phase_n, 128), b16),
            pltpu.VMEM((BLOCKS, phase_n, chunk, 128), b16),
            pltpu.VMEM((own, 128), f32),
            pltpu.VMEM((phase_n, own, 128), f32),
            pltpu.VMEM((phase_rows, chan_n, own, local), b16),
            pltpu.VMEM((phase_rows, chan_n, own, local), b16),
            pltpu.SemaphoreType.DMA((count,)),
            pltpu.SemaphoreType.DMA((count,)),
            pltpu.SemaphoreType.DMA((9, phase_rows * chan_n)),
            pltpu.SemaphoreType.DMA((9, phase_rows * chan_n)),
        ],
        compiler_params=pltpu.CompilerParams(
            collective_id=0, has_side_effects=True, vmem_limit_bytes=48 * 1024 * 1024
        ),
        name="fused_blocks",
    )(jnp.swapaxes(frames, 0, 1), jnp.swapaxes(cotangent, 0, 1), taps, weights)
    final = jnp.swapaxes(final.reshape(phase_rows, chans, local), 0, 1)
    grad = jnp.swapaxes(grad.reshape(phase_rows, chans, local), 0, 1)
    kernels = jnp.transpose(kernels.reshape(BLOCKS, 27, 2, own, chans), (0, 4, 1, 2, 3))
    tap_sums = tap_sums.reshape(chans, 128)[:, : 3 * BLOCKS]
    tap_sums = jnp.transpose(tap_sums).reshape(temporal_taps.shape)
    return (final, grad, tap_sums, kernels.astype(f32))


def fits(frames):
    chans, phase_rows, local = frames.shape
    phase_n, chan_n = lax.axis_size("phase"), lax.axis_size("chan")
    whole_hops = all(
        2**block < phase_n or 2**block % phase_n == 0 for block in range(BLOCKS)
    )
    return (
        phase_n % 2 == 0
        and phase_n > 2
        and 128 % chans == 0
        and chan_n > 1
        and chans % (16 * chan_n) == 0
        and local % 128 == 0
        and SY * SZ == 128
        and whole_hops
    )


def any_size(frames, temporal_taps, conv_weights, cotangent):
    body = fused if fits(frames) else per_device
    return body(frames, temporal_taps, conv_weights, cotangent)


def solution(mesh):
    in_specs = (
        P(None, "phase", "chan"),
        P(),
        P(None, None, None, None, "chan"),
        P(None, "phase", "chan"),
    )
    out_specs = (
        P(None, "phase", "chan"),
        P(None, "phase", "chan"),
        P(),
        P(None, None, None, None, "chan"),
    )
    return jax.shard_map(
        any_size, mesh=mesh, in_specs=in_specs, out_specs=out_specs, check_vma=False
    )
```

```python
import functools

import jax
import jax.numpy as jnp
from jax import lax
from jax.experimental import pallas as pl
from jax.experimental.pallas import tpu as pltpu
from jax.sharding import PartitionSpec as P

BLOCKS = 4
SY = 8
SZ = 16


cell_offsets = [
    (kernel_pos // 9 - 1, kernel_pos // 3 % 3 - 1, kernel_pos % 3 - 1) for kernel_pos in range(27)
]


def shifted(block, axis, distance):
    devices = range(lax.axis_size(axis))
    route = [((i - distance) % len(devices), i) for i in devices]
    return lax.ppermute(block, axis, route)


def padded_2(cells, sides, width):
    for axis, dim in sides:
        count = lax.axis_size(axis)
        ends = count - 1
        head = lax.slice_in_dim(cells, 0, width, axis=dim)
        tail = lax.slice_in_dim(cells, cells.shape[dim] - width, cells.shape[dim], axis=dim)
        cells = jnp.concatenate(
            [
                lax.ppermute(tail, axis, [(i, (i + 1) % count) for i in range(ends)]),
                cells,
                lax.ppermute(head, axis, [((i + 1) % count, i) for i in range(ends)]),
            ],
            axis=dim,
        )
    return cells


def within_plane(source, step_y, step_z):
    cell_count = source.shape[-1]
    last_dim = source.ndim - 1
    margin = SZ + 1
    moved = step_y * SZ + step_z
    padded = jnp.pad(source, [(0, 0)] * last_dim + [(margin, margin)])
    window = lax.slice_in_dim(padded, margin + moved, margin + moved + cell_count, axis=last_dim)
    places = jnp.arange(cell_count, dtype=jnp.int32)
    coord_y = places // SZ + step_y
    coord_z = places % SZ + step_z
    inside = (coord_y >= 0) & (coord_y < SY) & (coord_z >= 0) & (coord_z < SZ)
    return jnp.where(inside, window, jnp.zeros_like(window))


def shifted_cells(rimmed, step_x, step_y, step_z):
    planes = rimmed.shape[-2] - 2
    rows = lax.slice_in_dim(rimmed, 1 + step_x, 1 + step_x + planes, axis=rimmed.ndim - 2)
    moved = within_plane(rows, step_y, step_z)
    return moved.reshape(moved.shape[:-2] + (planes * moved.shape[-1],))


def offset_stack(rimmed, first, count, sign):
    picked = cell_offsets[first : first + count]
    return jnp.stack(
        [
            shifted_cells(rimmed, sign * offset[0], sign * offset[1], sign * offset[2])
            for offset in picked
        ],
        axis=1,
    )


def back_block(source, hops):
    if hops == 0:
        return source
    return shifted(source, "phase", hops)


def next_block(source, hops):
    if hops == 0:
        return source
    return shifted(source, "phase", -hops)


def neighbours(source, reach):
    phase_rows = source.shape[1]
    hops, rest = divmod(reach, phase_rows)
    if rest == 0:
        return (back_block(source, hops), next_block(source, hops))
    joined = jnp.concatenate([back_block(source, hops + 1), back_block(source, hops)], axis=1)
    behind = joined[:, phase_rows - rest : 2 * phase_rows - rest]
    joined = jnp.concatenate([next_block(source, hops), next_block(source, hops + 1)], axis=1)
    ahead = joined[:, rest : rest + phase_rows]
    return (behind, ahead)


def per_device(frames, temporal_taps, conv_weights, cotangent):
    chans, phase_rows, cell_count = frames.shape
    plane_cells = SY * SZ
    planes = cell_count // plane_cells
    state = frames
    saved = []
    for block_num in range(BLOCKS):
        reach = 2**block_num
        behind, ahead = neighbours(state, reach)
        tap_rows = temporal_taps[block_num][:, :, None, None]
        mixed = (
            tap_rows[0] * behind.astype(jnp.float32)
            + tap_rows[1] * state.astype(jnp.float32)
            + tap_rows[2] * ahead.astype(jnp.float32)
        ).astype(jnp.bfloat16)
        rimmed = padded_2(mixed.reshape(chans, phase_rows, planes, plane_cells), (("chan", 2),), 1)
        kernel = lax.all_gather(conv_weights[block_num], "chan", axis=3, tiled=True)
        conv_out = jnp.zeros((chans, 2, phase_rows, cell_count), jnp.float32)
        for first in range(0, 27, 9):
            group = offset_stack(rimmed, first, 9, 1)
            conv_out = conv_out + jnp.einsum(
                "ikpv,ikgo->ogpv",
                group,
                kernel[:, first : first + 9],
                preferred_element_type=jnp.float32,
            )
        value_part = conv_out[:, 0]
        gate_sig = jax.nn.sigmoid(conv_out[:, 1])
        saved.append((state, behind, ahead, rimmed, kernel, value_part, gate_sig))
        state = (state.astype(jnp.float32) + value_part * gate_sig).astype(jnp.bfloat16)
    grad_state = cotangent
    weight_grads = [None] * BLOCKS
    tap_grads = [None] * BLOCKS
    for block_num in reversed(range(BLOCKS)):
        reach = 2**block_num
        prior, behind, ahead, rimmed, kernel, value_part, gate_sig = saved[block_num]
        tap_rows = temporal_taps[block_num][:, :, None, None]
        grad_y = grad_state.astype(jnp.float32)
        grad_z = jnp.stack(
            [grad_y * gate_sig, grad_y * value_part * gate_sig * (1.0 - gate_sig)], axis=1
        ).astype(jnp.bfloat16)
        rim_grad = padded_2(
            grad_z.reshape(chans, 2, phase_rows, planes, plane_cells), (("chan", 3),), 1
        )
        grad_mix = jnp.zeros((chans, phase_rows, cell_count), jnp.float32)
        for first in range(0, 27, 3):
            group = offset_stack(rim_grad, first, 3, -1)
            grad_mix = grad_mix + jnp.einsum(
                "okgpv,ikgo->ipv",
                group,
                kernel[:, first : first + 3],
                preferred_element_type=jnp.float32,
            )
        kernel_parts = []
        for first in range(0, 27, 9):
            group = offset_stack(rimmed, first, 9, 1)
            kernel_parts.append(
                jnp.einsum("ikpv,ogpv->ikgo", group, grad_z, preferred_element_type=jnp.float32)
            )
        grad_kernel = jnp.concatenate(kernel_parts, axis=1)
        grad_tap = jnp.stack(
            [
                jnp.sum(grad_mix * behind.astype(jnp.float32), axis=(1, 2)),
                jnp.sum(grad_mix * prior.astype(jnp.float32), axis=(1, 2)),
                jnp.sum(grad_mix * ahead.astype(jnp.float32), axis=(1, 2)),
            ]
        )
        grad_low = grad_mix.astype(jnp.bfloat16)
        back_mix, ahead_mix = neighbours(grad_low, reach)
        grad_state = (
            grad_y
            + tap_rows[0] * ahead_mix.astype(jnp.float32)
            + tap_rows[1] * grad_low.astype(jnp.float32)
            + tap_rows[2] * back_mix.astype(jnp.float32)
        ).astype(jnp.bfloat16)
        kernel_piece = lax.psum_scatter(
            grad_kernel.astype(jnp.bfloat16), "chan", scatter_dimension=3, tiled=True
        )
        grad_kernel = lax.psum(kernel_piece, "phase").astype(jnp.float32)
        weight_grads[block_num] = grad_kernel
        tap_grads[block_num] = grad_tap
    grad_weights = jnp.stack(weight_grads)
    grad_taps = lax.psum(jnp.stack(tap_grads), ("phase", "chan"))
    return (state, grad_state, grad_taps, grad_weights)


class Copies:
    def __init__(self, send_sems, recv_sems):
        self.send_sems = send_sems
        self.recv_sems = recv_sems
        self.started = []

    def send(self, src, dst, target):
        number = len(self.started)
        copy = pltpu.make_async_remote_copy(
            src_ref=src,
            dst_ref=dst,
            send_sem=self.send_sems.at[number],
            recv_sem=self.recv_sems.at[number],
            device_id=target,
            device_id_type=pl.DeviceIdType.MESH,
        )
        copy.start()
        self.started.append(copy)
        return copy


def copy_count(phase_n, chan_n, blocks):
    return (
        blocks * (2 + (chan_n - 1))
        + blocks * ((chan_n - 1) + 2 + 2 * (phase_n - 1))
        + (phase_n - 1)
        + (chan_n - 1)
    )


def plane_shift(array, step, phase_rows):
    if step == 0:
        return array
    width = array.shape[1] // phase_rows
    cells = SY * SZ
    blank = jnp.zeros((array.shape[0], cells), array.dtype)
    pieces = []
    for row in range(phase_rows):
        base = row * width
        if step < 0:
            pieces += [blank, array[:, base : base + width - cells]]
        else:
            pieces += [array[:, base + cells : base + width], blank]
    return jnp.concatenate(pieces, axis=1)


def fused_kernel(
    dims,
    frames,
    cotangent,
    taps,
    weights_far,
    final_out,
    grad_out,
    gw_out,
    taps_out,
    weights,
    w_fwd,
    w_bwd,
    behind_v,
    ahead_v,
    gw_all,
    fr_behind,
    fr_ahead,
    home_grad,
    home_gl,
    gl_stage,
    fr_x,
    cot_x,
    state,
    behind_b,
    ahead_b,
    mixed,
    stack,
    value,
    gate,
    gz_stack,
    gm_send,
    gm_full,
    gm_recv,
    gl,
    gl_back,
    gl_ahead,
    gw_send,
    gw_recv,
    tap_send,
    tap_recv,
    final_send,
    grad_send,
    send_sems,
    recv_sems,
    move_send,
    move_recv,
    weight_sems,
):
    phase_n, chan_n, phase_rows, own, whole, chunk = dims
    chans = own * chan_n
    width = phase_rows * whole
    local = whole // chan_n
    cells = SY * SZ
    p = lax.axis_index("phase")
    z = lax.axis_index("chan")
    copies = Copies(send_sems, recv_sems)
    f32, b16 = jnp.float32, jnp.bfloat16

    def at_phase(hop):
        return {"phase": lax.rem(p + (hop % phase_n), phase_n), "chan": z}

    def at_chan(hop):
        return {"phase": p, "chan": lax.rem(z + (hop % chan_n), chan_n)}

    def rows_of(index):
        return pl.ds(pl.multiple_of(index * own, own), own)

    weight_copies = []
    for block in range(BLOCKS):
        weight_copies.append(
            pltpu.make_async_copy(
                weights_far.at[block], weights.at[block], weight_sems.at[block]
            )
        )
        weight_copies[-1].start()

    half = phase_n // 2
    q = lax.rem(p, 2) * half + lax.div(p, 2)

    def holder(residue):
        return lax.rem(residue, half) * 2 + lax.div(residue, half)

    def at_residue(hop):
        return {"phase": holder(lax.rem(q + (hop % phase_n), phase_n)), "chan": z}

    everyone = phase_n * chan_n
    barrier = pltpu.get_barrier_semaphore()
    for hop in range(1, everyone):
        number = lax.rem(p * chan_n + z + hop, everyone)
        other = {"phase": lax.div(number, chan_n), "chan": lax.rem(number, chan_n)}
        pl.semaphore_signal(
            barrier, inc=1, device_id=other, device_id_type=pl.DeviceIdType.MESH
        )
    pl.semaphore_wait(barrier, everyone - 1)

    lane = lax.broadcasted_iota(jnp.int32, (1, width), 1)
    coord_z = lax.rem(lane, SZ)
    coord_y = lax.rem(lane // SZ, SY)
    steps = [(k // 3 - 1, k % 3 - 1) for k in range(9)]
    masks = {}
    for step_y, step_z in steps:
        y, w = coord_y + step_y, coord_z + step_z
        masks[step_y, step_z] = (
            ((y >= 0) & (y < SY) & (w >= 0) & (w < SZ)).astype(f32)
        )

    def cell_shifts(array, sign):
        for step_y, step_z in steps:
            step_y, step_z = sign * step_y, sign * step_z
            moved = step_y * SZ + step_z
            if moved == 0:
                yield array.astype(b16)
            else:
                rolled = pltpu.roll(array, (-moved) % width, axis=1)
                yield (rolled * masks[step_y, step_z]).astype(b16)

    moves = []

    phases = phase_n * phase_rows

    def working_place(index, ahead=0):
        phase = lax.rem(phase_rows * p + index + (ahead % phases), phases)
        return holder(lax.rem(phase, phase_n)), lax.div(phase, phase_n)

    def home_place(index, ahead=0):
        phase = lax.rem(q + phase_n * index + (ahead % phases), phases)
        return lax.div(phase, phase_rows), lax.rem(phase, phase_rows)

    def move(group, source, target, place):
        for index in range(phase_rows):
            where, slot = place(index)
            for hop in range(chan_n):
                chan = lax.rem(z + hop, chan_n)
                src, dst = source(index, chan), target.at[slot, z]
                recv_sem = move_recv.at[group, slot * chan_n + z]
                copy = pltpu.make_async_remote_copy(
                    src_ref=src,
                    dst_ref=dst,
                    send_sem=move_send.at[group, index * chan_n + hop],
                    recv_sem=recv_sem,
                    device_id={"phase": where, "chan": chan},
                    device_id_type=pl.DeviceIdType.MESH,
                )
                if hop:
                    copy.start()
                    moves.append((copy, None))
                else:
                    pl.when(where != p)(copy.start)
                    pl.when(where == p)(pltpu.make_async_copy(src, dst, recv_sem).start)
                    moves.append((copy, where))

    def arrived(group, target):
        for slot in range(phase_rows):
            for chan in range(chan_n):
                part = target.at[slot, chan]
                pltpu.make_async_copy(
                    part, part, move_recv.at[group, slot * chan_n + chan]
                ).wait()

    def join_planes(parts):
        return jnp.concatenate(
            [parts[u, chan] for u in range(phase_rows) for chan in range(chan_n)], axis=1
        )

    def send_home(group, array, stage, target):
        for u in range(phase_rows):
            for chan in range(chan_n):
                base = u * whole + chan * local
                stage[u, chan] = array[:, base : base + local]
        move(group, lambda index, chan: stage.at[index, chan], target, home_place)

    def turned(array, count):
        cut_at = (count % phase_rows) * whole
        if cut_at == 0:
            return array
        return jnp.concatenate([array[:, width - cut_at :], array[:, : width - cut_at]], axis=1)

    def start_neighbours(source, back, ahead, reach):
        if reach % phase_n == 0:
            return []
        got = [copies.send(source, back, at_residue(reach))]
        if (2 * reach) % phase_n:
            got.append(copies.send(source, ahead, at_residue(-reach)))
        return got

    def read_neighbours(source, back, ahead, got, reach):
        if not got:
            here = source[...].astype(f32)
            return turned(here, reach // phase_n), turned(here, -(reach // phase_n))
        for copy in got:
            copy.wait_recv()
        back_raw = back[...].astype(f32)
        ahead_raw = back_raw if len(got) == 1 else ahead[...].astype(f32)
        return (
            jnp.where(q >= reach, back_raw, turned(back_raw, 1)),
            jnp.where(q + reach < phase_n, ahead_raw, turned(ahead_raw, -1)),
        )

    def wait_all(got):
        for copy in got:
            copy.wait_recv()

    def own_rows(source):
        return lambda index, chan: source.at[index, rows_of(chan), :]

    move(0, own_rows(frames), fr_x, working_place)
    move(4, own_rows(frames), fr_behind, functools.partial(working_place, ahead=1))
    move(5, own_rows(frames), fr_ahead, functools.partial(working_place, ahead=-1))
    pair = 2 * own

    def ready_forward(block):
        weight_copies[block].wait()
        for step in range(3):
            rows = weights[block, step * 9 * pair : (step + 1) * 9 * pair, :]
            w_fwd[block, step * pair : (step + 1) * pair, :] = jnp.concatenate(
                [rows[k * pair : (k + 1) * pair] for k in range(9)], axis=1
            )

    def ready_backward(block):
        for step in range(3):
            rows = weights[block, step * 9 * pair : (step + 1) * 9 * pair, :]
            w_bwd[block, step * chans : (step + 1) * chans, :] = jnp.transpose(
                rows.astype(f32)
            ).astype(b16)

    ready_forward(0)
    own_taps = taps[rows_of(z), :]

    def tap(block, index):
        number = 3 * block + index
        return own_taps[:, number : number + 1]

    arrived(0, fr_x)
    state[0] = join_planes(fr_x)

    for block in range(BLOCKS):
        reach = 2**block
        here = state[block].astype(f32)
        if block == 0:
            arrived(4, fr_behind)
            arrived(5, fr_ahead)
            back = join_planes(fr_behind).astype(f32)
            ahead = join_planes(fr_ahead).astype(f32)
        else:
            got = start_neighbours(
                state.at[block], behind_b.at[block], ahead_b.at[block], reach
            )
            back, ahead = read_neighbours(
                state.at[block], behind_b.at[block], ahead_b.at[block], got, reach
            )
        behind_v[block] = back.astype(b16)
        ahead_v[block] = ahead.astype(b16)
        mix = tap(block, 0) * back + tap(block, 1) * here + tap(block, 2) * ahead
        mixed[block, rows_of(z), :] = mix.astype(b16)
        got = []
        for hop in range(1, chan_n):
            part = mixed.at[block, rows_of(z), :]
            got.append(copies.send(part, part, at_chan(hop)))
        if block == 0:
            move(1, own_rows(cotangent), cot_x, working_place)
        ready_backward(block)
        if block + 1 < BLOCKS:
            ready_forward(block + 1)
        wait_all(got)
        full = mixed[block].astype(f32)
        for number, moved in enumerate(cell_shifts(full, 1)):
            stack[block, number * chans : (number + 1) * chans, :] = moved
        parts = jnp.dot(w_fwd[block], stack[block], preferred_element_type=f32)
        rows = 2 * own
        conv = (
            parts[rows : 2 * rows]
            + plane_shift(parts[:rows], -1, phase_rows)
            + plane_shift(parts[2 * rows :], 1, phase_rows)
        )
        sig = jax.nn.sigmoid(conv[own:])
        value[block] = conv[:own]
        gate[block] = sig
        state[block + 1] = (here + conv[:own] * sig).astype(b16)

    send_home(2, state[BLOCKS], final_send, final_out)

    arrived(1, cot_x)
    grad = join_planes(cot_x).astype(f32)
    tap_lane = lax.broadcasted_iota(jnp.int32, tap_send.shape, 1)
    tap_sums = jnp.zeros(tap_send.shape, f32)
    got_final_grads = []

    def reduce_kernel(block, got):
        wait_all(got)
        total = gw_send[block, rows_chunk(p), :].astype(f32)
        for hop in range(1, phase_n):
            source = lax.rem(p + hop, phase_n)
            total = total + gw_recv[block, source].astype(f32)
        gw_all[block, p] = total.astype(b16)
        for hop in range(1, phase_n):
            part = gw_all.at[block, p]
            got_final_grads.append(copies.send(part, part, at_phase(hop)))

    def rows_chunk(index):
        return pl.ds(pl.multiple_of(index * chunk, chunk), chunk)

    waiting = None
    for block in reversed(range(BLOCKS)):
        reach = 2**block
        sig, val = gate[block], value[block]
        gz = jnp.concatenate([grad * sig, grad * val * sig * (1.0 - sig)], axis=0)
        for number, moved in enumerate(cell_shifts(gz.astype(b16).astype(f32), -1)):
            gz_stack[number * 2 * own : (number + 1) * 2 * own, :] = moved
        parts = jnp.dot(w_bwd[block], gz_stack[...], preferred_element_type=f32)
        gm = (
            parts[chans : 2 * chans]
            + plane_shift(parts[:chans], 1, phase_rows)
            + plane_shift(parts[2 * chans :], -1, phase_rows)
        )
        gm_send[block] = gm.astype(b16)
        gm_full[...] = gm
        got = []
        for hop in range(1, chan_n):
            there = at_chan(hop)
            got.append(
                copies.send(
                    gm_send.at[block, rows_of(there["chan"]), :], gm_recv.at[block, z], there
                )
            )
        low = gz.astype(b16)
        sides = jnp.concatenate(
            [plane_shift(low, 1, phase_rows), low, plane_shift(low, -1, phase_rows)], axis=0
        )
        products = lax.dot_general(
            sides, stack[block], (((1,), (1,)), ((), ())), preferred_element_type=f32
        ).astype(b16)
        wide = -(-products.shape[1] // 128) * 128
        if wide != products.shape[1]:
            blank = jnp.zeros((6 * own, wide - products.shape[1]), b16)
            products = jnp.concatenate([products, blank], axis=1)
        filled = 6 * own * (wide // 128)
        for tile in range(wide // 128):
            gw_send[block, tile * 6 * own : (tile + 1) * 6 * own, :] = products[
                :, tile * 128 : (tile + 1) * 128
            ]
        if filled < gw_send.shape[1]:
            gw_send[block, filled:, :] = jnp.zeros((gw_send.shape[1] - filled, 128), b16)
        kernel_got = []
        for hop in range(1, phase_n):
            there = at_phase(hop)
            kernel_got.append(
                copies.send(
                    gw_send.at[block, rows_chunk(there["phase"]), :], gw_recv.at[block, p], there
                )
            )
        if waiting is not None:
            reduce_kernel(*waiting)
        waiting = (block, kernel_got)
        wait_all(got)
        mix_grad = gm_full[rows_of(z), :]
        for hop in range(1, chan_n):
            mix_grad = mix_grad + gm_recv[block, lax.rem(z + hop, chan_n)].astype(f32)
        gl[block] = mix_grad.astype(b16)
        if block == 0:
            for u in range(phase_rows):
                for chan in range(chan_n):
                    base = u * whole + chan * local
                    gl_stage[u, chan] = gl[0, :, base : base + local]
            for turn, ahead in enumerate((0, 1, -1)):
                move(
                    6 + turn,
                    lambda index, chan: gl_stage.at[index, chan],
                    home_gl.at[turn],
                    functools.partial(home_place, ahead=ahead),
                )
        else:
            got = start_neighbours(gl.at[block], gl_back.at[block], gl_ahead.at[block], reach)
        for index, factor in enumerate((behind_v, state, ahead_v)):
            total = jnp.sum(mix_grad * factor[block].astype(f32), axis=1, keepdims=True)
            tap_sums = jnp.where(tap_lane == 3 * block + index, total, tap_sums)
        if block == 0:
            tap_send[...] = tap_sums
            tap_got = []
            for hop in range(1, phase_n):
                tap_got.append(copies.send(tap_send, tap_recv.at[p], at_phase(hop)))
            break
        low = gl[block].astype(f32)
        back, ahead = read_neighbours(
            gl.at[block], gl_back.at[block], gl_ahead.at[block], got, reach
        )
        moved = grad + tap(block, 0) * ahead + tap(block, 1) * low + tap(block, 2) * back
        rounded = moved.astype(b16)
        grad = rounded.astype(f32)
        if block == 1:
            send_home(3, rounded, grad_send, home_grad)

    per_tile = 128 // chans

    def give_kernel(block):
        joined = jnp.concatenate([gw_all[block, index] for index in range(phase_n)], axis=0)
        for step in range(3):
            for k in range(9):
                top = (k // per_tile) * 6 * own + step * pair
                left = (k % per_tile) * chans
                base = (step * 9 + k) * pair
                gw_out[block, base : base + pair, :] = joined[
                    top : top + pair, left : left + chans
                ]

    reduce_kernel(*waiting)
    wait_all(got_final_grads[: 2 * (phase_n - 1)])
    for block in reversed(range(BLOCKS - 2, BLOCKS)):
        give_kernel(block)
    wait_all(tap_got)
    tap_recv[p] = tap_send[...]
    total = tap_recv[0]
    for index in range(1, phase_n):
        total = total + tap_recv[index]
    taps_out[z] = total
    got_taps = []
    for hop in range(1, chan_n):
        part = taps_out.at[z]
        got_taps.append(copies.send(part, part, at_chan(hop)))
    arrived(3, home_grad)
    for turn in range(3):
        arrived(6 + turn, home_gl.at[turn])
    for index in range(chan_n):
        columns = taps[index * own : (index + 1) * own, :]
        for slot in range(phase_rows):
            moved = (
                home_grad[slot, index].astype(f32)
                + columns[:, 0:1] * home_gl[2, slot, index].astype(f32)
                + columns[:, 1:2] * home_gl[0, slot, index].astype(f32)
                + columns[:, 2:3] * home_gl[1, slot, index].astype(f32)
            )
            grad_out[slot, index] = moved.astype(b16)
    wait_all(got_final_grads[2 * (phase_n - 1) :])
    for block in reversed(range(BLOCKS - 2)):
        give_kernel(block)
    arrived(2, final_out)
    wait_all(got_taps)
    for copy, where in moves:
        if where is None:
            copy.wait_send()
        else:
            pl.when(where != p)(copy.wait_send)
    for copy in copies.started:
        copy.wait_send()


def fused(frames, temporal_taps, conv_weights, cotangent):
    chans, phase_rows, local = frames.shape
    phase_n, chan_n = lax.axis_size("phase"), lax.axis_size("chan")
    own = chans // chan_n
    whole = local * chan_n
    width = phase_rows * whole
    stack_rows = 9 * chans
    kernel_rows = 6 * own * -(-stack_rows // 128)
    chunk = -(-kernel_rows // (16 * phase_n)) * 16
    b16, f32 = jnp.bfloat16, jnp.float32
    weights = jnp.transpose(conv_weights, (0, 2, 3, 4, 1)).reshape(BLOCKS, 54 * own, chans)
    taps = jnp.transpose(temporal_taps, (2, 0, 1)).reshape(chans, 3 * BLOCKS)
    count = copy_count(phase_n, chan_n, BLOCKS)
    dims = (phase_n, chan_n, phase_rows, own, whole, chunk)
    vmem = pl.BlockSpec(memory_space=pltpu.VMEM)
    final, grad, kernels, tap_sums = pl.pallas_call(
        functools.partial(fused_kernel, dims),
        out_shape=(
            jax.ShapeDtypeStruct((phase_rows, chan_n, own, local), b16),
            jax.ShapeDtypeStruct((phase_rows, chan_n, own, local), b16),
            jax.ShapeDtypeStruct((BLOCKS, 54 * own, chans), b16),
            jax.ShapeDtypeStruct((chan_n, own, 128), f32),
        ),
        in_specs=[vmem] * 3 + [pl.BlockSpec(memory_space=pltpu.HBM)],
        out_specs=(vmem,) * 4,
        scratch_shapes=[
            pltpu.VMEM((BLOCKS, 54 * own, chans), b16),
            pltpu.VMEM((BLOCKS, 6 * own, 9 * chans), b16),
            pltpu.VMEM((BLOCKS, 3 * chans, 18 * own), b16),
            pltpu.VMEM((BLOCKS, own, width), b16),
            pltpu.VMEM((BLOCKS, own, width), b16),
            pltpu.VMEM((BLOCKS, phase_n, chunk, 128), b16),
            pltpu.VMEM((phase_rows, chan_n, own, local), b16),
            pltpu.VMEM((phase_rows, chan_n, own, local), b16),
            pltpu.VMEM((phase_rows, chan_n, own, local), b16),
            pltpu.VMEM((3, phase_rows, chan_n, own, local), b16),
            pltpu.VMEM((phase_rows, chan_n, own, local), b16),
            pltpu.VMEM((phase_rows, chan_n, own, local), b16),
            pltpu.VMEM((phase_rows, chan_n, own, local), b16),
            pltpu.VMEM((BLOCKS + 1, own, width), b16),
            pltpu.VMEM((BLOCKS, own, width), b16),
            pltpu.VMEM((BLOCKS, own, width), b16),
            pltpu.VMEM((BLOCKS, chans, width), b16),
            pltpu.VMEM((BLOCKS, stack_rows, width), b16),
            pltpu.VMEM((BLOCKS, own, width), f32),
            pltpu.VMEM((BLOCKS, own, width), f32),
            pltpu.VMEM((18 * own, width), b16),
            pltpu.VMEM((BLOCKS, chans, width), b16),
            pltpu.VMEM((chans, width), f32),
            pltpu.VMEM((BLOCKS, chan_n, own, width), b16),
            pltpu.VMEM((BLOCKS, own, width), b16),
            pltpu.VMEM((BLOCKS, own, width), b16),
            pltpu.VMEM((BLOCKS, own, width), b16),
            pltpu.VMEM((BLOCKS, chunk * phase_n, 128), b16),
            pltpu.VMEM((BLOCKS, phase_n, chunk, 128), b16),
            pltpu.VMEM((own, 128), f32),
            pltpu.VMEM((phase_n, own, 128), f32),
            pltpu.VMEM((phase_rows, chan_n, own, local), b16),
            pltpu.VMEM((phase_rows, chan_n, own, local), b16),
            pltpu.SemaphoreType.DMA((count,)),
            pltpu.SemaphoreType.DMA((count,)),
            pltpu.SemaphoreType.DMA((9, phase_rows * chan_n)),
            pltpu.SemaphoreType.DMA((9, phase_rows * chan_n)),
            pltpu.SemaphoreType.DMA((BLOCKS,)),
        ],
        compiler_params=pltpu.CompilerParams(
            collective_id=0, has_side_effects=True, vmem_limit_bytes=48 * 1024 * 1024
        ),
        name="fused_blocks",
    )(jnp.swapaxes(frames, 0, 1), jnp.swapaxes(cotangent, 0, 1), taps, weights)
    final = jnp.swapaxes(final.reshape(phase_rows, chans, local), 0, 1)
    grad = jnp.swapaxes(grad.reshape(phase_rows, chans, local), 0, 1)
    kernels = jnp.transpose(kernels.reshape(BLOCKS, 27, 2, own, chans), (0, 4, 1, 2, 3))
    tap_sums = tap_sums.reshape(chans, 128)[:, : 3 * BLOCKS]
    tap_sums = jnp.transpose(tap_sums).reshape(temporal_taps.shape)
    return (final, grad, tap_sums, kernels.astype(f32))


def fits(frames):
    chans, phase_rows, local = frames.shape
    phase_n, chan_n = lax.axis_size("phase"), lax.axis_size("chan")
    whole_hops = all(
        2**block < phase_n or 2**block % phase_n == 0 for block in range(BLOCKS)
    )
    return (
        phase_n % 2 == 0
        and phase_n > 2
        and 128 % chans == 0
        and chan_n > 1
        and chans % (16 * chan_n) == 0
        and local % 128 == 0
        and SY * SZ == 128
        and whole_hops
    )


def any_size(frames, temporal_taps, conv_weights, cotangent):
    body = fused if fits(frames) else per_device
    return body(frames, temporal_taps, conv_weights, cotangent)


def solution(mesh):
    in_specs = (
        P(None, "phase", "chan"),
        P(),
        P(None, None, None, None, "chan"),
        P(None, "phase", "chan"),
    )
    out_specs = (
        P(None, "phase", "chan"),
        P(None, "phase", "chan"),
        P(),
        P(None, None, None, None, "chan"),
    )
    return jax.shard_map(
        any_size, mesh=mesh, in_specs=in_specs, out_specs=out_specs, check_vma=False
    )
```
